512 devices in a mesh: row: 16 (over z, core), col: 32 (over x, y).
Axes of the slice: x: 4, y: 8, z: 8, core: 2. Of those that a mesh axis runs over, the one named last changes fastest.
Arguments:
- tokens_in: bfloat16 [320, 6144], P('col', 'row'), may hold values from -6 to 6
- layer_norm_gain: float32 [6144], P('row'), may hold values from 0.5 to 1.5
- w_qkv: bfloat16 [6144, 3, 4096], P('row', None, 'col'), may hold values from -0.063788795 to 0.063788795
- qk_gain: float32 [2, 4096], P(None, 'col'), may hold values from 0.6 to 3.75
- w_up: bfloat16 [6144, 24576], P('row', 'col'), may hold values from -0.078125 to 0.078125
- w_attn_out: bfloat16 [4096, 6144], P('col', 'row'), may hold values from -0.09375 to 0.09375
- w_down: bfloat16 [24576, 6144], P('col', 'row'), may hold values from -0.0390625 to 0.0390625
- cotangent: bfloat16 [320, 6144], P('col', 'row'), may hold values from -6 to 6
Outputs:
- layer_out: bfloat16 [320, 6144], P('col', 'row')
- token_input_gradient: bfloat16 [320, 6144], P('col', 'row')
- layer_norm_gain_gradient: float32 [6144], P('row')
- d_w_qkv: bfloat16 [6144, 3, 4096], P('row', None, 'col')
- d_qk_gain: float32 [2, 4096], P(None, 'col')
- d_w_up: bfloat16 [6144, 24576], P('row', 'col')
- d_w_attn_out: bfloat16 [4096, 6144], P('col', 'row')
- d_w_down: bfloat16 [24576, 6144], P('col', 'row')
The draws below stay inside these ranges and needn't reach their ends.
All inputs are finite; a program needn't handle non-finite values.
Results may differ from the reference program's by a relative error of at most 0.022.
Values may be sent and summed in bfloat16 or wider, within the bound.
No kernel may reach another device: no remote copies, remote signals or barrier semaphores. Data moves between devices by JAX's collectives and lax.ppermute only.
A program may use at most 64 MiB of HBM per device.

```python
import jax
import jax.numpy as jnp
from jax import lax

MODEL_DIMENSION = 6144
FF = 24576
HEADS = 32
HEAD_DIM = 128
TOKENS = 320


def draw_w_qkv(key, part):
    key = jax.random.fold_in(key, 11)
    limit = 4.9 * MODEL_DIMENSION ** (-0.5)
    base = jax.random.normal(key, (MODEL_DIMENSION, 3, HEADS * HEAD_DIM), jnp.float32) * MODEL_DIMENSION ** (-0.5)
    return jnp.clip(base, -limit, limit).astype(jnp.bfloat16)


def draw_qk_gain(key, part):
    key = jax.random.fold_in(key, 17)
    return jax.random.uniform(key, (2, HEADS * HEAD_DIM), jnp.float32, 0.6, 1.6)


def shard_levels(rng, dims, cuts, least, largest):
    gain, own = 1.0, jax.random.fold_in(rng, 6)
    for dim, blocks in cuts:
        draws = jnp.exp(jax.random.uniform(jax.random.fold_in(own, dim), (blocks,), jnp.float32, least / len(cuts), largest / len(cuts)))
        gain = gain * jnp.repeat(draws, dims[dim] // blocks).reshape([-1 if axis == dim else 1 for axis in range(len(dims))])
    return gain


def bell_draw(rng, extent, scale, most, pieces=(), held_as=jnp.bfloat16):
    factor_of = shard_levels(rng, extent, pieces, -0.22, 0.18) if pieces else 1.0
    drawn = jax.random.normal(rng, extent, jnp.float32) * scale * factor_of
    return jnp.minimum(jnp.maximum(drawn, -most), most).astype(held_as)


def setup_inputs(seed: int = 0) -> dict:
    key_list = jax.random.split(jax.random.key(seed), 9)
    return {
        "tokens_in": bell_draw(key_list[0], (TOKENS, MODEL_DIMENSION), 1.0, 6.0, ((0, 32), (1, 16))),
        "layer_norm_gain": jnp.clip(1.0 + 0.1 * jax.random.normal(key_list[1], (MODEL_DIMENSION,), jnp.float32), 0.5, 1.5),
        "w_qkv": draw_w_qkv(jax.random.fold_in(key_list[8], 71), 0),
        "qk_gain": draw_qk_gain(jax.random.fold_in(key_list[8], 71), 0),
        "w_up": bell_draw(key_list[4], (MODEL_DIMENSION, FF), MODEL_DIMENSION ** -0.5, 0.078125, ((0, 16), (1, 32))),
        "w_attn_out": bell_draw(key_list[5], (HEADS * HEAD_DIM, MODEL_DIMENSION), (HEADS * HEAD_DIM) ** -0.5, 0.09375, ((0, 32), (1, 16))),
        "w_down": bell_draw(key_list[6], (FF, MODEL_DIMENSION), FF ** -0.5, 0.0390625, ((0, 32), (1, 16))),
        "cotangent": bell_draw(key_list[7], (TOKENS, MODEL_DIMENSION), 1.0, 6.0, ((0, 32), (1, 16))),
    }


def qk_norm(values, gain_vec):
    centred = values - lax.optimization_barrier(jnp.mean(values, -1, keepdims=True))
    variance = lax.optimization_barrier(jnp.mean(centred * centred, -1, keepdims=True))
    return centred * lax.rsqrt(variance + 1e-06) * gain_vec.reshape(values.shape[1], values.shape[2])

def reference(tokens_in, layer_norm_gain, w_qkv, qk_gain, w_up, w_attn_out, w_down, cotangent):
    head_w = HEADS * HEAD_DIM
    score_scale = HEAD_DIM ** (-0.5)
    input_single_precision = tokens_in.astype(jnp.float32)
    token_row_average = lax.optimization_barrier(jnp.sum(input_single_precision, 1)) / MODEL_DIMENSION
    variance = lax.optimization_barrier(jnp.sum(input_single_precision * input_single_precision, 1)) / MODEL_DIMENSION - token_row_average * token_row_average
    inverse_deviation = lax.rsqrt(variance + 1e-06)
    centered_scaled_input = (input_single_precision - token_row_average[:, None]) * inverse_deviation[:, None]
    normalized_tokens = (centered_scaled_input * layer_norm_gain).astype(jnp.bfloat16)
    w_in = jnp.concatenate([w_qkv.reshape(MODEL_DIMENSION, 3 * head_w), w_up], 1)
    merged = jnp.dot(normalized_tokens, w_in, preferred_element_type=jnp.float32)
    query = merged[:, :head_w].reshape(TOKENS, HEADS, HEAD_DIM)
    key_pre = merged[:, head_w:2 * head_w].reshape(TOKENS, HEADS, HEAD_DIM)
    v_rows = merged[:, 2 * head_w:3 * head_w].astype(jnp.bfloat16).reshape(TOKENS, HEADS, HEAD_DIM)
    up_rows = merged[:, 3 * head_w:]
    q_normed, q_back = jax.vjp(qk_norm, query, qk_gain[0])
    k_normed, k_back = jax.vjp(qk_norm, key_pre, qk_gain[1])
    q_rows = q_normed.astype(jnp.bfloat16)
    k_rows = k_normed.astype(jnp.bfloat16)
    scores = jnp.einsum('qhd,khd->hqk', q_rows.astype(jnp.float32), k_rows.astype(jnp.float32)) * score_scale
    probs = jax.nn.softmax(scores, -1)
    prob_low = probs.astype(jnp.bfloat16)
    attended = jnp.einsum('hqk,khd->qhd', prob_low.astype(jnp.float32), v_rows.astype(jnp.float32))
    attended = attended.astype(jnp.bfloat16).reshape(TOKENS, head_w)
    hidden_f, gelu_back = jax.vjp(jax.nn.gelu, up_rows)
    hidden = hidden_f.astype(jnp.bfloat16)
    joined = jnp.concatenate([attended, hidden], 1)
    w_cat = jnp.concatenate([w_attn_out, w_down], 0)
    layer_out = (input_single_precision + jnp.dot(joined, w_cat, preferred_element_type=jnp.float32)).astype(jnp.bfloat16)
    d_cat = jnp.dot(joined.T, cotangent, preferred_element_type=jnp.float32)
    d_w_attn_out = d_cat[:head_w].astype(jnp.bfloat16)
    d_w_down = d_cat[head_w:].astype(jnp.bfloat16)
    d_joined = jnp.dot(cotangent, w_cat.T, preferred_element_type=jnp.float32)
    d_attended = d_joined[:, :head_w].astype(jnp.bfloat16).reshape(TOKENS, HEADS, HEAD_DIM)
    d_hidden = d_joined[:, head_w:].astype(jnp.bfloat16)
    d_up = gelu_back(d_hidden.astype(jnp.float32))[0].astype(jnp.bfloat16)
    d_probs = jnp.einsum('qhd,khd->hqk', d_attended.astype(jnp.float32), v_rows.astype(jnp.float32))
    row_delta = lax.optimization_barrier(jnp.sum(probs * d_probs, -1, keepdims=True))
    d_scores = (probs * (d_probs - row_delta)).astype(jnp.bfloat16).astype(jnp.float32)
    d_qn = jnp.einsum('hqk,khd->qhd', d_scores, k_rows.astype(jnp.float32)) * score_scale
    d_kn = jnp.einsum('hqk,qhd->khd', d_scores, q_rows.astype(jnp.float32)) * score_scale
    d_value = jnp.einsum('hqk,qhd->khd', prob_low.astype(jnp.float32), d_attended.astype(jnp.float32))
    d_query, d_q_gain = q_back(d_qn)
    d_key, d_k_gain = k_back(d_kn)
    d_merged = jnp.concatenate([d_query.astype(jnp.bfloat16).reshape(TOKENS, head_w), d_key.astype(jnp.bfloat16).reshape(TOKENS, head_w), d_value.astype(jnp.bfloat16).reshape(TOKENS, head_w), d_up], 1)
    d_w_in = jnp.dot(normalized_tokens.T, d_merged, preferred_element_type=jnp.float32)
    d_w_qkv = d_w_in[:, :3 * head_w].reshape(MODEL_DIMENSION, 3, head_w).astype(jnp.bfloat16)
    d_w_up = d_w_in[:, 3 * head_w:].astype(jnp.bfloat16)
    normalized_rows_gradient = jnp.dot(d_merged, w_in.T, preferred_element_type=jnp.float32)
    layer_norm_gain_gradient = lax.optimization_barrier(jnp.sum(normalized_rows_gradient * centered_scaled_input, 0))
    centered_scaled_gradient = normalized_rows_gradient * layer_norm_gain
    gradient_row_total = lax.optimization_barrier(jnp.sum(centered_scaled_gradient, 1, keepdims=True))
    gradient_dot_product = lax.optimization_barrier(jnp.sum(centered_scaled_gradient * centered_scaled_input, 1, keepdims=True))
    token_input_gradient = (cotangent.astype(jnp.float32) + (centered_scaled_gradient - gradient_row_total / MODEL_DIMENSION - centered_scaled_input * gradient_dot_product / MODEL_DIMENSION) * inverse_deviation[:, None]).astype(jnp.bfloat16)
    d_qk_gain = jnp.stack([d_q_gain, d_k_gain])
    return (layer_out, token_input_gradient, layer_norm_gain_gradient, d_w_qkv, d_qk_gain, d_w_up, d_w_attn_out, d_w_down)
```

```python
import jax
import jax.numpy as jnp
from jax import lax
from jax.sharding import Mesh
from jax.sharding import PartitionSpec as P

HEAD_DIM = 128
EPS = 1e-06
ROW = ("z", "core")
COL = ("x", "y")
F32 = jnp.float32
BF16 = jnp.bfloat16


def split(values, parts):
    out = []
    for _ in range(parts):
        high = lax.reduce_precision(values, 8, 7)
        out.append(high.astype(BF16))
        values = values - high
    return out


def dot(a, b, dims):
    return lax.dot_general(a, b, (dims, ((), ())), preferred_element_type=F32)


NN = ((1,), (0,))
NT = ((1,), (1,))
TN = ((0,), (0,))


def lane_pad(values, width):
    return jnp.pad(values, [(0, 0)] * (values.ndim - 1) + [(0, width - values.shape[-1])])


def shards(tokens_in, gain, w_qkv, qk_gain, w_up, w_attn_out, w_down, cotangent):
    rows_c, width = tokens_in.shape
    n_col = lax.axis_size(COL)
    n_z = lax.axis_size("z")
    tokens = rows_c * n_col
    rows_z = tokens // n_z
    model_width = width * lax.axis_size(ROW)
    core = lax.axis_index("core")
    first = core == 0
    swap = [(0, 1), (1, 0)]
    scale = HEAD_DIM ** (-0.5)
    w_qkv2 = w_qkv.reshape(width, 3 * HEAD_DIM)

    mine = jnp.concatenate([tokens_in, cotangent], 0)
    got = lax.all_to_all(jnp.broadcast_to(mine, (n_col,) + mine.shape), COL, 0, 0)
    x_all = got[:, :rows_c].reshape(tokens, width)
    cot_all = got[:, rows_c:].reshape(tokens, width)

    x_f = x_all.astype(F32)
    sum_1 = jnp.sum(x_f, 1)
    sum_2 = jnp.sum(x_f * x_f, 1)
    gain_parts = jnp.stack(split(gain, 3) + [jnp.zeros((width,), BF16)] * 5)
    xg = jnp.concatenate([(x_f * gain).astype(BF16), gain_parts], 0)
    p_qkv = dot(xg, w_qkv2, NN)
    p_up = dot(xg, w_up, NN)
    p_da = dot(cot_all, w_attn_out, NT)
    p_dh = dot(cot_all, w_down, NT)
    c_qkv = jnp.sum(p_qkv[tokens:], 0)
    c_up = jnp.sum(p_up[tokens:], 0)
    p_qkv, p_up = p_qkv[:tokens], p_up[:tokens]
    q4 = 2 * HEAD_DIM
    zero = jnp.zeros((q4,), F32)
    lay_0 = jnp.concatenate([p_qkv, p_da, p_up[:, :q4], p_dh[:, :q4]], 1)
    lay_1 = jnp.concatenate(
        [p_up[:, q4 : 2 * q4], p_dh[:, q4 : 2 * q4], p_up[:, 2 * q4 :], p_dh[:, 2 * q4 :]], 1
    )
    c_0 = jnp.concatenate([c_qkv, zero[:HEAD_DIM], c_up[:q4], zero])
    c_1 = jnp.concatenate([c_up[q4 : 2 * q4], zero, c_up[2 * q4 :], zero])
    wide = lay_0.shape[1]

    def extras(c_vec, s_1, s_2, c_h):
        rows = split(c_vec, 2)
        for s, c in zip(split(s_1, 3), split(c_h, 3)):
            rows.append(
                jnp.concatenate(
                    [lane_pad(s, 512), lane_pad(c, wide - 512)]
                )
            )
        rows += [lane_pad(s, wide) for s in split(s_2, 3)]
        return jnp.stack(rows)

    def unpack(block):
        block = block.astype(F32)
        h = jnp.sum(block[2:5], 0)
        return (
            jnp.sum(block[0:2], 0),
            h[:tokens],
            jnp.sum(block[5:8], 0)[:tokens],
            h[512 : 512 + 3 * HEAD_DIM],
        )

    own = jnp.where(first, lay_0, lay_1)
    other = jnp.where(first, lay_1, lay_0).astype(BF16)
    c_own = jnp.where(first, c_0, c_1)
    c_other = jnp.where(first, c_1, c_0)

    sent = jnp.concatenate([other, extras(c_other, sum_1, sum_2, c_qkv)], 0)
    came = lax.ppermute(sent, "core", swap)
    half = (own + came[:tokens].astype(F32)).astype(BF16)
    o_c, o_1, o_2, o_h = unpack(came[tokens:])
    extra = extras(c_own + o_c, sum_1 + o_1, sum_2 + o_2, c_qkv + o_h)
    sent = jnp.concatenate(
        [half.reshape(n_z, rows_z, wide), jnp.broadcast_to(extra, (n_z,) + extra.shape)], 1
    )
    total = jnp.sum(lax.all_to_all(sent, "z", 0, 0).astype(F32), 0)
    c_tot, s_1, s_2, c_h = unpack(total[rows_z:])
    total = total[:rows_z]

    mean = s_1 / model_width
    inv = lax.rsqrt(s_2 / model_width - mean * mean + EPS)
    at = lax.axis_index("z") * rows_z
    mean_z = lax.dynamic_slice(mean, (at,), (rows_z,))[:, None]
    inv_z = lax.dynamic_slice(inv, (at,), (rows_z,))[:, None]
    merged = (total - mean_z * c_tot) * inv_z

    def mlp(up, d_hidden, c_vec):
        hidden, back = jax.vjp(jax.nn.gelu, up)
        d_up = back(d_hidden.astype(BF16).astype(F32))[0].astype(BF16)
        d_f = d_up.astype(F32)
        return hidden.astype(BF16), d_up, jnp.sum(d_f * c_vec, 1), jnp.sum(d_f * up, 1)

    def norm(values, g):
        average = jnp.mean(values, -1, keepdims=True)
        centred = values - average
        rstd = lax.rsqrt(jnp.mean(centred * centred, -1, keepdims=True) + EPS)
        return (centred * rstd * g).astype(BF16), rstd[:, 0], average[:, 0]

    h_a, u_a, s1_a, s2_a = mlp(merged[:, :q4], total[:, q4 : 2 * q4], c_tot[:q4])
    h_b, u_b, s1_b, s2_b = mlp(merged[:, 2 * q4 : 3 * q4], total[:, 3 * q4 :], c_tot[2 * q4 : 3 * q4])
    q_z, rstd_q, mean_q = norm(merged[:, :HEAD_DIM], qk_gain[0])
    k_z, rstd_k, mean_k = norm(merged[:, HEAD_DIM : 2 * HEAD_DIM], qk_gain[1])
    v_z = merged[:, 2 * HEAD_DIM : 3 * HEAD_DIM].astype(BF16)
    da_z = total[:, 3 * HEAD_DIM : 4 * HEAD_DIM].astype(BF16)
    left = jnp.where(
        first, jnp.concatenate([q_z, k_z, v_z, da_z], 1), jnp.concatenate([h_a, u_a], 1)
    )
    e_cols = jnp.stack(
        [rstd_q, rstd_k, mean_q, mean_k, jnp.where(first, 0, s1_a) + s1_b, jnp.where(first, 0, s2_a) + s2_b],
        1,
    )
    e_cols = lane_pad(jnp.concatenate(split(e_cols, 2), 1), HEAD_DIM)
    sent = jnp.concatenate([left, h_b, u_b, e_cols], 1)

    mine = lax.all_to_all(jnp.broadcast_to(sent, (n_z,) + sent.shape), "z", 0, 0)
    mine = mine.reshape(tokens, sent.shape[1])
    theirs = lax.ppermute(mine, "core", swap)
    a0 = jnp.where(first, mine, theirs)
    a1 = jnp.where(first, theirs, mine)
    q_rows, k_rows, v_rows, d_att = (
        a0[:, i * HEAD_DIM : (i + 1) * HEAD_DIM] for i in range(4)
    )
    hidden = jnp.concatenate([a0[:, 2 * q4 : 3 * q4], a1[:, :q4], a1[:, 2 * q4 : 3 * q4]], 1)
    d_up = jnp.concatenate([a0[:, 3 * q4 : 4 * q4], a1[:, q4 : 2 * q4], a1[:, 3 * q4 : 4 * q4]], 1)
    e0 = a0[:, wide:].astype(F32)
    e1 = a1[:, wide:].astype(F32)
    e0 = e0[:, :6] + e0[:, 6:12]
    e1 = e1[:, :6] + e1[:, 6:12]
    rstd_q, rstd_k, mean_q, mean_k = (e0[:, i : i + 1] for i in range(4))

    probs = jax.nn.softmax(dot(q_rows, k_rows, NT) * scale, -1)
    prob_low = probs.astype(BF16)
    attended = dot(prob_low, v_rows, NN).astype(BF16)
    branch = dot(attended, w_attn_out, NN) + dot(hidden, w_down, NN)
    d_probs = dot(d_att, v_rows, NT)
    row_delta = jnp.sum(probs * d_probs, -1, keepdims=True)
    d_scores = (probs * (d_probs - row_delta)).astype(BF16)
    d_qn = dot(d_scores, k_rows, NN) * scale
    d_kn = dot(d_scores, q_rows, TN) * scale
    d_value = dot(prob_low, d_att, TN)

    def norm_back(rows, rstd, average, g, d_rows):
        unit = rows.astype(F32) / g
        d_unit = d_rows * g
        d_values = (
            d_unit
            - jnp.mean(d_unit, -1, keepdims=True)
            - unit * jnp.mean(d_unit * unit, -1, keepdims=True)
        ) * rstd
        return d_values.astype(BF16), jnp.sum(d_rows * unit, 0), unit / rstd + average

    d_q, d_q_gain, query = norm_back(q_rows, rstd_q, mean_q, qk_gain[0], d_qn)
    d_k, d_k_gain, key = norm_back(k_rows, rstd_k, mean_k, qk_gain[1], d_kn)
    d_qk_gain = jnp.stack([d_q_gain, d_k_gain])
    d_qkv = jnp.concatenate([d_q, d_k, d_value.astype(BF16)], 1)
    d_f = d_qkv.astype(F32)
    t_1 = jnp.sum(d_f * c_h, 1) + e0[:, 4] + e1[:, 4]
    t_2 = (
        jnp.sum(d_f * jnp.concatenate([query, key, v_rows.astype(F32)], 1), 1) + e0[:, 5] + e1[:, 5]
    )
    d_normed = dot(d_qkv, w_qkv2, NT) + dot(d_up, w_up, NT)
    xhat = (x_f - mean[:, None]) * inv[:, None]
    normed = (xhat * gain).astype(BF16)
    part_gain = jnp.sum(d_normed * xhat, 0)
    d_w_qkv = dot(normed, d_qkv, TN).astype(BF16).reshape(w_qkv.shape)
    d_w_up = dot(normed, d_up, TN).astype(BF16)
    d_w_attn_out = dot(attended, cot_all, TN).astype(BF16)
    d_w_down = dot(hidden, cot_all, TN).astype(BF16)

    send = jnp.concatenate([branch.astype(BF16), d_normed.astype(BF16)], 1)
    send = send.reshape(n_col, rows_c, 2 * width)
    rows = [
        jnp.concatenate([g, lane_pad(s, width)])
        for g, s in zip(split(part_gain, 3), split(t_1, 3))
    ] + [jnp.concatenate([jnp.zeros((width,), BF16), lane_pad(s, width)]) for s in split(t_2, 3)]
    rows = jnp.stack(rows)
    send = jnp.concatenate([send, jnp.broadcast_to(rows, (n_col,) + rows.shape)], 1)
    total = jnp.sum(lax.all_to_all(send, COL, 0, 0).astype(F32), 0)
    layer_out = (tokens_in.astype(F32) + total[:rows_c, :width]).astype(BF16)
    d_gain = jnp.sum(total[rows_c : rows_c + 3, :width], 0)
    t_1 = jnp.sum(total[rows_c : rows_c + 3, width:], 0)
    t_2 = jnp.sum(total[rows_c + 3 : rows_c + 6, width:], 0)
    at = lax.axis_index(COL) * rows_c
    t_1, t_2, mean_c, inv_c = (
        lax.dynamic_slice(v, (at,), (rows_c,))[:, None] for v in (t_1, t_2, mean, inv)
    )
    xhat_c = (tokens_in.astype(F32) - mean_c) * inv_c
    d_xhat = total[:rows_c, width:] * gain
    token_grad = (
        cotangent.astype(F32) + (d_xhat - t_1 / model_width - xhat_c * t_2 / model_width) * inv_c
    ).astype(BF16)
    return (
        layer_out,
        token_grad,
        d_gain,
        d_w_qkv,
        d_qk_gain,
        d_w_up,
        d_w_attn_out,
        d_w_down,
    )


def solution(mesh):
    fine = Mesh(mesh.devices.reshape(-1, 2, 4, 8), ("z", "core", "x", "y"))
    in_specs = (
        P(COL, ROW),
        P(ROW),
        P(ROW, None, COL),
        P(None, COL),
        P(ROW, COL),
        P(COL, ROW),
        P(COL, ROW),
        P(COL, ROW),
    )
    out_specs = (
        P(COL, ROW),
        P(COL, ROW),
        P(ROW),
        P(ROW, None, COL),
        P(None, COL),
        P(ROW, COL),
        P(COL, ROW),
        P(COL, ROW),
    )
    return jax.shard_map(shards, mesh=fine, in_specs=in_specs, out_specs=out_specs, check_vma=False)
```

```python
import jax
import jax.numpy as jnp
from jax import lax
from jax.experimental import pallas as pl
from jax.experimental.pallas import tpu as pltpu
from jax.sharding import Mesh
from jax.sharding import PartitionSpec as P

HEAD = 128
QUARTER = 256
WIDE = 1024
EXTRA = 8
PACK = WIDE + HEAD
EPS = 1e-06
ROW = ("z", "core")
COL = ("x", "y")
F32 = jnp.float32
BF16 = jnp.bfloat16

NN = (((1,), (0,)), ((), ()))
NT = (((1,), (1,)), ((), ()))
TN = (((0,), (0,)), ((), ()))


def dot(a, b, dims):
    return lax.dot_general(a, b, dims, preferred_element_type=F32)


def split(values, parts):
    out = []
    for _ in range(parts):
        high = values.astype(BF16).astype(F32)
        out.append(high)
        values = values - high
    return out


def one_hot(rows, lanes, first):
    lane = lax.broadcasted_iota(jnp.int32, (rows, lanes), 1)
    return lane == lax.broadcasted_iota(jnp.int32, (rows, lanes), 0) + first


def to_column(row, hot):
    return jnp.sum(jnp.where(hot, row, 0.0), 1, keepdims=True)


def to_row(column, hot):
    return jnp.sum(jnp.where(hot, column, 0.0), 0, keepdims=True)


def call(kernel, outs, scratch, *args):
    return pl.pallas_call(
        kernel,
        out_shape=outs,
        in_specs=[pl.BlockSpec(memory_space=pltpu.VMEM)] * len(args),
        out_specs=[pl.BlockSpec(memory_space=pltpu.VMEM)] * len(outs),
        scratch_shapes=scratch,
        compiler_params=pltpu.CompilerParams(vmem_limit_bytes=40 * 2**20),
    )(*args)


def shape(dims, dtype=BF16):
    return jax.ShapeDtypeStruct(dims, dtype)


def spread_kernel(x_ref, cot_ref, out_ref, block):
    rows = x_ref.shape[0]
    block[...] = jnp.zeros_like(block)
    block[0:rows] = x_ref[...].astype(F32)
    block[rows : 2 * rows] = cot_ref[...].astype(F32)
    out_ref[...] = jnp.broadcast_to(block[...].astype(BF16)[None], out_ref.shape)


def product_kernel(
    got_ref, gain_ref, wq_ref, wu_ref, wa_ref, wd_ref, own_ref, other_ref, x_ref, cot_ref, xs, cs, lay
):
    n_col, rows = got_ref.shape[0], x_ref.shape[0] // got_ref.shape[0]
    tokens = x_ref.shape[0]
    for c in range(n_col):
        both = got_ref[c].astype(F32)
        xs[c * rows : (c + 1) * rows, :] = both[0:rows]
        cs[c * rows : (c + 1) * rows, :] = both[rows : 2 * rows]
    x = xs[0:tokens, :]
    gain = gain_ref[...]
    xs[tokens:, :] = jnp.concatenate(split(gain, 3) + [jnp.zeros((5, gain.shape[1]), F32)], 0)
    x_low = x.astype(BF16)
    x_ref[...] = x_low
    cot = cs[...].astype(BF16)
    cot_ref[...] = cot
    xg = jnp.concatenate([x * gain, xs[tokens:, :]], 0).astype(BF16)
    core = lax.axis_index("core")

    p = dot(xg, wq_ref[...], NN)
    lay[0, 0:tokens, 0 : 3 * HEAD] = p[0:tokens]
    c_qkv = jnp.sum(p[tokens:], 0, keepdims=True)
    p = dot(xg, wu_ref[...], NN)
    lay[0, 0:tokens, 512:768] = p[0:tokens, 0:256]
    lay[1, 0:tokens, 0:256] = p[0:tokens, 256:512]
    lay[1, 0:tokens, 512:768] = p[0:tokens, 512:768]
    c_up = jnp.sum(p[tokens:], 0, keepdims=True)
    lay[0, 0:tokens, 384:512] = dot(cot, wa_ref[...], NT)
    p = dot(cot, wd_ref[...], NT)
    lay[0, 0:tokens, 768:1024] = p[:, 0:256]
    lay[1, 0:tokens, 256:512] = p[:, 256:512]
    lay[1, 0:tokens, 768:1024] = p[:, 512:768]

    ones = jnp.ones((8, x.shape[1]), BF16)
    square = x * x
    high = square.astype(BF16)
    low = (square - high.astype(F32)).astype(BF16)
    s_1 = dot(ones, x_low, NT)[0:1]
    s_2 = (dot(ones, high, NT) + dot(ones, low, NT))[0:1]
    fill = jnp.zeros((1, 512 - tokens), F32)
    blank = jnp.zeros((1, 256), F32)
    mixed = jnp.concatenate([s_1, fill, c_qkv, blank[:, 0:128]], 1)
    s_2 = jnp.concatenate([s_2, fill, blank, blank], 1)
    c_0 = jnp.concatenate([c_qkv, blank[:, 0:128], c_up[:, 0:256], blank], 1)
    c_1 = jnp.concatenate([c_up[:, 256:512], blank, c_up[:, 512:768], blank], 1)
    zeros = jnp.zeros((5, WIDE), F32)
    lay[0, tokens:, :] = jnp.concatenate([c_0, mixed, s_2, zeros], 0)
    lay[1, tokens:, :] = jnp.concatenate([c_1, mixed, s_2, zeros], 0)
    own_ref[...] = lay[core]
    other_ref[0:tokens, :] = lay[1 - core, 0:tokens, :].astype(BF16)
    c_other = lay[1 - core, tokens : tokens + 1, :]
    other_ref[tokens:, :] = jnp.concatenate(
        split(c_other, 2) + split(mixed, 3) + split(s_2, 3), 0
    ).astype(BF16)


def half_kernel(own_ref, came_ref, out_ref):
    n_z, rows = out_ref.shape[0], out_ref.shape[1] - EXTRA
    tokens = n_z * rows
    parts = came_ref[tokens:, :].astype(F32)
    own = own_ref[tokens:, :]
    c_vec = own[0:1] + parts[0:1] + parts[1:2]
    mixed = own[1:2] + jnp.sum(parts[2:5], 0, keepdims=True)
    s_2 = own[2:3] + jnp.sum(parts[5:8], 0, keepdims=True)
    extra = jnp.concatenate(split(c_vec, 2) + split(mixed, 3) + split(s_2, 3), 0).astype(BF16)
    for d in range(n_z):
        at = pl.ds(d * rows, rows)
        out_ref[d, 0:rows, :] = (own_ref[at, :] + came_ref[at, :].astype(F32)).astype(BF16)
        out_ref[d, rows:, :] = extra


def gelu_parts(x):
    c = 0.7978845608028654
    t = jnp.tanh(c * (x + 0.044715 * (x * x * x)))
    half = 0.5 * (1.0 + t)
    slope = half + 0.5 * x * (1.0 - t * t) * (c * (1.0 + 3 * 0.044715 * (x * x)))
    return x * half, slope


def row_kernel(model_width, got_ref, qk_gain_ref, out_ref, stats_ref):
    n_z, rows = got_ref.shape[0], got_ref.shape[1] - EXTRA
    total = got_ref[0].astype(F32)
    for d in range(1, n_z):
        total = total + got_ref[d].astype(F32)
    c_tot = jnp.sum(total[rows : rows + 2], 0, keepdims=True)
    mixed = jnp.sum(total[rows + 2 : rows + 5], 0, keepdims=True)
    mean = mixed[:, 0:384] / model_width
    var = jnp.sum(total[rows + 5 :, 0:384], 0, keepdims=True) / model_width - mean * mean
    inv = lax.rsqrt(var + EPS)
    stats_ref[...] = jnp.concatenate([mean, inv, mixed[:, 512:896], jnp.zeros((5, 384), F32)], 0)
    hot = one_hot(rows, 384, lax.axis_index("z") * rows)
    mean_z, inv_z = to_column(mean, hot), to_column(inv, hot)
    total = total[0:rows]

    def columns(at, size):
        return (total[:, at : at + size] - mean_z * c_tot[:, at : at + size]) * inv_z

    def mlp(at):
        up = columns(at, 256)
        hidden, slope = gelu_parts(up)
        d_up = (total[:, at + 256 : at + 512].astype(BF16).astype(F32) * slope).astype(BF16)
        d_f = d_up.astype(F32)
        return (
            hidden.astype(BF16),
            d_up,
            jnp.sum(d_f * c_tot[:, at : at + 256], 1, keepdims=True),
            jnp.sum(d_f * up, 1, keepdims=True),
        )

    def norm(at, g):
        values = columns(at, HEAD)
        average = jnp.mean(values, -1, keepdims=True)
        centred = values - average
        rstd = lax.rsqrt(jnp.mean(centred * centred, -1, keepdims=True) + EPS)
        return (centred * rstd * g).astype(BF16), rstd, average

    lane = lax.broadcasted_iota(jnp.int32, (rows, HEAD), 1)

    def pack(values):
        out = jnp.zeros((rows, HEAD), F32)
        for i, v in enumerate(values):
            high = v.astype(BF16).astype(F32)
            out = jnp.where(lane == i, high, out)
            out = jnp.where(lane == i + 8, v - high, out)
        return out.astype(BF16)

    def store(at, value):
        out_ref[:, :, at : at + value.shape[1]] = jnp.broadcast_to(value[None], (n_z, *value.shape))

    hidden, d_up, s1_b, s2_b = mlp(512)
    store(512, hidden)
    store(768, d_up)
    core = lax.axis_index("core")

    @pl.when(core == 0)
    def _():
        q, rstd_q, mean_q = norm(0, qk_gain_ref[0:1])
        k, rstd_k, mean_k = norm(HEAD, qk_gain_ref[1:2])
        store(0, q)
        store(HEAD, k)
        store(2 * HEAD, columns(2 * HEAD, HEAD).astype(BF16))
        store(3 * HEAD, total[:, 3 * HEAD : 4 * HEAD].astype(BF16))
        store(WIDE, pack([rstd_q, rstd_k, mean_q, mean_k, s1_b, s2_b]))

    @pl.when(core != 0)
    def _():
        hidden, d_up, s1_a, s2_a = mlp(0)
        store(0, hidden)
        store(256, d_up)
        none = jnp.zeros_like(s1_a)
        store(WIDE, pack([none, none, none, none, s1_a + s1_b, s2_a + s2_b]))


def attention_kernel(
    mine_ref, theirs_ref, stats_ref, x_ref, gain_ref, qk_gain_ref, wq_ref, wu_ref, wa_ref, wd_ref,
    send_ref, d_gain_ref, hidden_ref, d_up_ref, att_ref, d_qkv_ref, normed_ref, both, block
):
    n_col = send_ref.shape[0]
    tokens, width = x_ref.shape
    rows = tokens // n_col
    core = lax.axis_index("core")
    both[core] = mine_ref[...]
    both[1 - core] = theirs_ref[...]
    hidden_ref[:, 0:256] = both[0, :, 512:768]
    hidden_ref[:, 256:512] = both[1, :, 0:256]
    hidden_ref[:, 512:768] = both[1, :, 512:768]
    d_up_ref[:, 0:256] = both[0, :, 768:1024]
    d_up_ref[:, 256:512] = both[1, :, 256:512]
    d_up_ref[:, 512:768] = both[1, :, 768:1024]
    scale = HEAD ** (-0.5)
    q, k, v, d_att = (both[0, :, i * HEAD : (i + 1) * HEAD] for i in range(4))
    e = both[0, :, WIDE:].astype(F32)
    e1 = both[1, :, WIDE:].astype(F32)

    def scalar(i):
        return e[:, i : i + 1] + e[:, i + 8 : i + 9]

    def scalar1(i):
        return e1[:, i : i + 1] + e1[:, i + 8 : i + 9]

    scores = dot(q, k, NT) * scale
    top = jnp.max(scores, -1, keepdims=True)
    probs = jnp.exp(scores - top)
    probs = probs / jnp.sum(probs, -1, keepdims=True)
    low = probs.astype(BF16)
    attended = dot(low, v, NN).astype(BF16)
    att_ref[...] = attended
    branch = dot(attended, wa_ref[...], NN) + dot(hidden_ref[...], wd_ref[...], NN)
    d_probs = dot(d_att, v, NT)
    delta = jnp.sum(probs * d_probs, -1, keepdims=True)
    d_scores = (probs * (d_probs - delta)).astype(BF16)
    d_qn = dot(d_scores, k, NN) * scale
    d_kn = dot(d_scores, q, TN) * scale
    d_v = dot(low, d_att, TN).astype(BF16)

    def back(rows_low, rstd, average, g, d_rows):
        unit = rows_low.astype(F32) / g
        d_unit = d_rows * g
        d_values = (
            d_unit
            - jnp.mean(d_unit, -1, keepdims=True)
            - unit * jnp.mean(d_unit * unit, -1, keepdims=True)
        ) * rstd
        return d_values.astype(BF16), jnp.sum(d_rows * unit, 0, keepdims=True), unit / rstd + average

    d_q, g_q, query = back(q, scalar(0), scalar(2), qk_gain_ref[0:1], d_qn)
    d_k, g_k, key = back(k, scalar(1), scalar(3), qk_gain_ref[1:2], d_kn)
    d_gain_ref[0:1, :] = g_q
    d_gain_ref[1:2, :] = g_k
    d_qkv_ref[:, 0:HEAD] = d_q
    d_qkv_ref[:, HEAD : 2 * HEAD] = d_k
    d_qkv_ref[:, 2 * HEAD :] = d_v
    d_normed = dot(d_qkv_ref[...], wq_ref[...], NT) + dot(d_up_ref[...], wu_ref[...], NT)

    c_h = stats_ref[2:3]
    d_qf, d_kf, d_vf = d_q.astype(F32), d_k.astype(F32), d_v.astype(F32)
    t_1 = scalar(4) + scalar1(4)
    t_1 += jnp.sum(d_qf * c_h[:, 0:HEAD] + d_kf * c_h[:, HEAD : 2 * HEAD] + d_vf * c_h[:, 2 * HEAD :], 1, keepdims=True)
    t_2 = scalar(5) + scalar1(5)
    t_2 += jnp.sum(d_qf * query + d_kf * key + d_vf * v.astype(F32), 1, keepdims=True)
    hot = one_hot(tokens, 384, 0)
    mean, inv = to_column(stats_ref[0:1], hot), to_column(stats_ref[1:2], hot)
    xhat = (x_ref[...].astype(F32) - mean) * inv
    normed_ref[...] = (xhat * gain_ref[...]).astype(BF16)
    part = split(jnp.sum(d_normed * xhat, 0, keepdims=True), 2)
    tail = jnp.concatenate(part + [to_row(t_1, hot), to_row(t_2, hot)], 0)
    block[0] = branch
    block[1] = d_normed
    for c in range(n_col):
        at = pl.ds(c * rows, rows)
        send_ref[c] = jnp.concatenate([block[0, at, :], block[1, at, :], tail], 0).astype(BF16)


def finish_kernel(
    model_width, got_ref, stats_ref, x_ref, cot_ref, gain_ref, out_ref, grad_ref, d_gain_ref
):
    rows = x_ref.shape[0]
    total = got_ref[0].astype(F32)
    for c in range(1, got_ref.shape[0]):
        total = total + got_ref[c].astype(F32)
    x = x_ref[...].astype(F32)
    out_ref[...] = (x + total[0:rows]).astype(BF16)
    d_gain_ref[...] = total[2 * rows : 2 * rows + 1] + total[2 * rows + 1 : 2 * rows + 2]
    col = lax.axis_index("x") * lax.axis_size("y") + lax.axis_index("y")
    hot = one_hot(rows, 384, col * rows)
    t_1 = to_column(total[2 * rows + 2 : 2 * rows + 3], hot)
    t_2 = to_column(total[2 * rows + 3 : 2 * rows + 4], hot)
    mean, inv = to_column(stats_ref[0:1], hot), to_column(stats_ref[1:2], hot)
    xhat = (x - mean) * inv
    d_xhat = total[rows : 2 * rows] * gain_ref[...]
    grad = (d_xhat - t_1 / model_width - xhat * t_2 / model_width) * inv
    grad_ref[...] = (cot_ref[...].astype(F32) + grad).astype(BF16)


def shards(tokens_in, gain, w_qkv, qk_gain, w_up, w_attn_out, w_down, cotangent):
    rows_c, width = tokens_in.shape
    n_col = lax.axis_size(COL)
    n_z = lax.axis_size("z")
    tokens = rows_c * n_col
    rows_z = tokens // n_z
    model_width = width * lax.axis_size(ROW)
    swap = [(0, 1), (1, 0)]
    hidden_w = w_up.shape[1]
    gain_row = gain.reshape(1, width)
    w_qkv2 = w_qkv.reshape(width, 3 * HEAD)
    chunk = 2 * rows_c + 4

    (spread,) = call(
        spread_kernel,
        [shape((n_col, chunk, width))],
        [pltpu.VMEM((chunk, width), F32)],
        tokens_in,
        cotangent,
    )
    got = lax.all_to_all(spread, COL, 0, 0)

    own, other, x_all, cot_all = call(
        product_kernel,
        [
            shape((tokens + EXTRA, WIDE), F32),
            shape((tokens + EXTRA, WIDE)),
            shape((tokens, width)),
            shape((tokens, width)),
        ],
        [
            pltpu.VMEM((tokens + EXTRA, width), F32),
            pltpu.VMEM((tokens, width), F32),
            pltpu.VMEM((2, tokens + EXTRA, WIDE), F32),
        ],
        got,
        gain_row,
        w_qkv2,
        w_up,
        w_attn_out,
        w_down,
    )
    came = lax.ppermute(other, "core", swap)
    (half,) = call(half_kernel, [shape((n_z, rows_z + EXTRA, WIDE))], [], own, came)
    got = lax.all_to_all(half, "z", 0, 0)

    packed, stats = call(
        lambda *refs: row_kernel(model_width, *refs),
        [shape((n_z, rows_z, PACK)), shape((8, width), F32)],
        [],
        got,
        qk_gain,
    )
    mine = lax.all_to_all(packed, "z", 0, 0).reshape(tokens, PACK)
    theirs = lax.ppermute(mine, "core", swap)

    send, d_qk_gain, hidden, d_up, attended, d_qkv, normed = call(
        attention_kernel,
        [
            shape((n_col, chunk, width)),
            shape((2, HEAD), F32),
            shape((tokens, hidden_w)),
            shape((tokens, hidden_w)),
            shape((tokens, HEAD)),
            shape((tokens, 3 * HEAD)),
            shape((tokens, width)),
        ],
        [pltpu.VMEM((2, tokens, PACK), BF16), pltpu.VMEM((2, tokens, width), F32)],
        mine,
        theirs,
        stats,
        x_all,
        gain_row,
        qk_gain,
        w_qkv2,
        w_up,
        w_attn_out,
        w_down,
    )
    got = lax.all_to_all(send, COL, 0, 0)
    d_w_qkv = dot(normed, d_qkv, TN).astype(BF16).reshape(w_qkv.shape)
    d_w_up = dot(normed, d_up, TN).astype(BF16)
    d_w_attn_out = dot(attended, cot_all, TN).astype(BF16)
    d_w_down = dot(hidden, cot_all, TN).astype(BF16)
    layer_out, token_grad, d_gain = call(
        lambda *refs: finish_kernel(model_width, *refs),
        [shape((rows_c, width)), shape((rows_c, width)), shape((1, width), F32)],
        [],
        got,
        stats,
        tokens_in,
        cotangent,
        gain_row,
    )
    return (
        layer_out,
        token_grad,
        d_gain.reshape(width),
        d_w_qkv,
        d_qk_gain,
        d_w_up,
        d_w_attn_out,
        d_w_down,
    )


def solution(mesh):
    fine = Mesh(mesh.devices.reshape(-1, 2, 4, 8), ("z", "core", "x", "y"))
    in_specs = (
        P(COL, ROW),
        P(ROW),
        P(ROW, None, COL),
        P(None, COL),
        P(ROW, COL),
        P(COL, ROW),
        P(COL, ROW),
        P(COL, ROW),
    )
    out_specs = (
        P(COL, ROW),
        P(COL, ROW),
        P(ROW),
        P(ROW, None, COL),
        P(None, COL),
        P(ROW, COL),
        P(COL, ROW),
        P(COL, ROW),
    )
    return jax.shard_map(shards, mesh=fine, in_specs=in_specs, out_specs=out_specs, check_vma=False)
```

```python
import jax
import jax.numpy as jnp
from jax import lax
from jax.experimental import pallas as pl
from jax.experimental.pallas import tpu as pltpu
from jax.sharding import Mesh
from jax.sharding import PartitionSpec as P

LANES = 128
EPS = 1e-06
ROW = ("z", "core")
COL = ("x", "y")
F32 = jnp.float32
BF16 = jnp.bfloat16

NN = (((1,), (0,)), ((), ()))
NT = (((1,), (1,)), ((), ()))
TN = (((0,), (0,)), ((), ()))


def dot(a, b, dims):
    return lax.dot_general(a, b, dims, preferred_element_type=F32)


def split(values, parts):
    out = []
    for _ in range(parts):
        high = values.astype(BF16).astype(F32)
        out.append(high)
        values = values - high
    return out


def one_hot(rows, lanes, first):
    lane = lax.broadcasted_iota(jnp.int32, (rows, lanes), 1)
    return lane == lax.broadcasted_iota(jnp.int32, (rows, lanes), 0) + first


def to_column(row, hot):
    return jnp.sum(jnp.where(hot, row, 0.0), 1, keepdims=True)


def to_row(column, hot):
    return jnp.sum(jnp.where(hot, column, 0.0), 0, keepdims=True)


def two_to_row(a, b, rows):
    out = jnp.zeros((1, LANES), F32)
    for at, part in zip((0, 32, 64, 96), split(a, 2) + split(b, 2)):
        out = out + to_row(part, one_hot(rows, LANES, at))
    return out


def two_to_columns(row, rows):
    first = one_hot(rows, LANES, 0) | one_hot(rows, LANES, 32)
    second = one_hot(rows, LANES, 64) | one_hot(rows, LANES, 96)
    return to_column(row, first), to_column(row, second)


def tile(j):
    return slice(j * LANES, (j + 1) * LANES)


def call(kernel, outs, scratch, *args):
    return pl.pallas_call(
        kernel,
        out_shape=outs,
        in_specs=[pl.BlockSpec(memory_space=pltpu.VMEM)] * len(args),
        out_specs=[pl.BlockSpec(memory_space=pltpu.VMEM)] * len(outs),
        scratch_shapes=scratch,
        compiler_params=pltpu.CompilerParams(vmem_limit_bytes=40 * 2**20),
    )(*args)


def shape(dims, dtype=BF16):
    return jax.ShapeDtypeStruct(dims, dtype)


def spread_kernel(x_any, cot_any, out_ref, x_ref, cot_ref, block, sems):
    copies = [
        pltpu.make_async_copy(x_any, x_ref, sems.at[0]),
        pltpu.make_async_copy(cot_any, cot_ref, sems.at[1]),
    ]
    for copy in copies:
        copy.start()
    block[...] = jnp.zeros_like(block)
    rows, width = x_ref.shape
    at = 0
    for copy, ref in zip(copies, (x_ref, cot_ref)):
        copy.wait()
        values = ref[...].astype(F32)
        for j in range(width // LANES):
            block[at : at + rows, :] = values[:, tile(j)]
            at += rows
    out_ref[...] = jnp.broadcast_to(block[...].astype(BF16)[None], out_ref.shape)


def product_kernel(
    got_ref, gain_ref, wq_ref, wu_ref, wa_ref, wd_ref,
    own_ref, other_ref, x_ref, cot_ref, xs, cs, ps, gs, st, lay
):
    tokens, width = x_ref.shape
    n_z = own_ref.shape[0]
    rows_c = tokens // got_ref.shape[0]
    rows = tokens // (2 * n_z)
    f_tiles, b_tiles = ps.shape[1] // LANES, gs.shape[1] // LANES
    f_sum = f_tiles * (rows + 1) + 3
    w_tiles = width // LANES
    for c in range(got_ref.shape[0]):
        values = got_ref[c].astype(F32)
        here = slice(c * rows_c, (c + 1) * rows_c)
        for j in range(w_tiles):
            xs[here, tile(j)] = values[j * rows_c : (j + 1) * rows_c]
            cs[here, tile(j)] = values[(w_tiles + j) * rows_c : (w_tiles + j + 1) * rows_c]
    x = xs[0:tokens, :]
    x_ref[...] = x.astype(BF16)
    cot = cs[...].astype(BF16)
    cot_ref[...] = cot
    gain = gain_ref[...]
    xs[tokens:, :] = jnp.concatenate(split(gain, 3) + [jnp.zeros((5, width), F32)], 0)
    xg = jnp.concatenate([x * gain, xs[tokens:, :]], 0).astype(BF16)
    ps[:, 0 : wq_ref.shape[1]] = dot(xg, wq_ref[...], NN)
    ps[:, wq_ref.shape[1] :] = dot(xg, wu_ref[...], NN)
    gs[:, 0 : wa_ref.shape[0]] = dot(cot, wa_ref[...], NT)
    gs[:, wa_ref.shape[0] :] = dot(cot, wd_ref[...], NT)
    c_vec = jnp.sum(ps[tokens:, :], 0, keepdims=True)
    s_1 = jnp.sum(x, 1, keepdims=True)
    s_2 = jnp.sum(x * x, 1, keepdims=True)
    lane = lax.broadcasted_iota(jnp.int32, (tokens, LANES), 1)
    place = lax.rem(lax.broadcasted_iota(jnp.int32, (tokens, LANES), 0), rows)
    st[...] = jnp.where(lane == place, s_1, 0.0) + jnp.where(lane == place + 32, s_2, 0.0)
    c_rows = jnp.concatenate([c_vec[:, tile(j)] for j in range(f_tiles)], 0)
    fill = jnp.zeros((lay.shape[2] - f_sum - b_tiles * rows, LANES), F32)
    for h in range(2):
        for d in range(n_z):
            at = slice((h * n_z + d) * rows, (h * n_z + d + 1) * rows)
            for j in range(f_tiles):
                lay[h, d, j * rows : (j + 1) * rows, :] = ps[at, tile(j)]
            stat = jnp.sum(st[at, :], 0, keepdims=True)
            lay[h, d, f_tiles * rows : f_sum, :] = jnp.concatenate([c_rows] + split(stat, 3), 0)
            for j in range(b_tiles):
                lay[h, d, f_sum + j * rows : f_sum + (j + 1) * rows, :] = gs[at, tile(j)]
            lay[h, d, f_sum + b_tiles * rows :, :] = fill
    core = lax.axis_index("core")
    own_ref[...] = lay[core]
    other_ref[...] = lay[1 - core].astype(BF16)


def add_kernel(f_sum, own_ref, came_ref, out_ref, block):
    for d in range(own_ref.shape[0]):
        block[...] = own_ref[d] + came_ref[d].astype(F32)
        stat = jnp.sum(block[f_sum - 3 : f_sum, :], 0, keepdims=True)
        block[f_sum - 3 : f_sum, :] = jnp.concatenate(split(stat, 3), 0)
        out_ref[d] = block[...].astype(BF16)


def gelu_parts(x):
    c = 0.7978845608028654
    t = jnp.tanh(c * (x + 0.044715 * (x * x * x)))
    half = 0.5 * (1.0 + t)
    slope = half + 0.5 * x * (1.0 - t * t) * (c * (1.0 + 3 * 0.044715 * (x * x)))
    return x * half, slope


def sum_blocks(got_ref, tot):
    total = got_ref[0].astype(F32)
    for d in range(1, got_ref.shape[0]):
        total = total + got_ref[d].astype(F32)
    tot[...] = total


def row_kernel(model_width, rows, f_sum, got_ref, qk_gain_ref, out_ref, c_ref, tot, block):
    sum_blocks(got_ref, tot)
    tiles = (f_sum - 3) // (rows + 1)
    c_ref[0:tiles, :] = tot[tiles * rows : tiles * rows + tiles, :]
    c_ref[tiles:, :] = jnp.zeros((c_ref.shape[0] - tiles, LANES), F32)
    stat = jnp.sum(tot[f_sum - 3 : f_sum, :], 0, keepdims=True)
    mean = to_column(stat, one_hot(rows, LANES, 0)) / model_width
    var = to_column(stat, one_hot(rows, LANES, 32)) / model_width - mean * mean
    inv = lax.rsqrt(var + EPS)

    def merged(j):
        return (tot[j * rows : (j + 1) * rows, :] - mean * c_ref[j : j + 1, :]) * inv

    def norm(j):
        values = merged(j)
        average = jnp.mean(values, -1, keepdims=True)
        centred = values - average
        rstd = lax.rsqrt(jnp.mean(centred * centred, -1, keepdims=True) + EPS)
        return centred * rstd * qk_gain_ref[j : j + 1], rstd, average

    block[0:rows, :], rstd_q, mean_q = norm(0)
    block[rows : 2 * rows, :], rstd_k, mean_k = norm(1)
    block[2 * rows : 3 * rows, :] = merged(2)
    back = tiles * rows
    block[back : back + rows, :] = tot[f_sum : f_sum + rows, :]
    s_1 = jnp.zeros((rows, LANES), F32)
    s_2 = jnp.zeros((rows, LANES), F32)
    for j in range(3, tiles):
        up = merged(j)
        hidden, slope = gelu_parts(up)
        block[j * rows : (j + 1) * rows, :] = hidden
        at = (j - 2) * rows
        d_hidden = tot[f_sum + at : f_sum + at + rows, :].astype(BF16).astype(F32)
        d_up = (d_hidden * slope).astype(BF16).astype(F32)
        block[back + at : back + at + rows, :] = d_up
        s_1 = s_1 + d_up * c_ref[j : j + 1, :]
        s_2 = s_2 + d_up * up
    s_1 = jnp.sum(s_1, 1, keepdims=True)
    s_2 = jnp.sum(s_2, 1, keepdims=True)
    last = (2 * tiles - 2) * rows
    pairs = ((rstd_q, rstd_k), (mean_q, mean_k), (mean, inv), (s_1, s_2))
    block[last:, :] = jnp.concatenate(
        [two_to_row(a, b, rows) for a, b in pairs]
        + [jnp.zeros((block.shape[0] - last - len(pairs), LANES), F32)],
        0,
    )
    out_ref[...] = jnp.broadcast_to(block[...].astype(BF16)[None], out_ref.shape)


def attention_kernel(
    rows, mine_ref, theirs_ref, c_ref, x_ref, gain_ref, qk_gain_ref, wq_ref, wu_ref, wa_ref, wd_ref,
    send_ref, d_gain_ref, att_ref, hidden_ref, d_qkv_ref, d_up_ref, normed_ref, stats_ref,
    both, cols, block
):
    n_z = mine_ref.shape[0]
    tokens, width = x_ref.shape
    half = tokens // 2
    core = lax.axis_index("core")
    tiles = both.shape[2] // LANES
    f_width = 3 * LANES + hidden_ref.shape[1]
    lane = lax.broadcasted_iota(jnp.int32, (rows, LANES), 1)
    for ref, h in ((mine_ref, core), (theirs_ref, 1 - core)):
        for d in range(n_z):
            values = ref[d].astype(F32)
            at = slice(d * rows, (d + 1) * rows)
            for j in range(tiles):
                both[h, at, tile(j)] = values[j * rows : (j + 1) * rows]
            scalars = jnp.zeros((rows, LANES), F32)
            for i in range(4):
                a, b = two_to_columns(values[tiles * rows + i : tiles * rows + i + 1], rows)
                scalars = jnp.where(lane == 2 * i, a, scalars)
                scalars = jnp.where(lane == 2 * i + 1, b, scalars)
            cols[h, at, :] = scalars

    def whole(at, size):
        return jnp.concatenate([both[h, :, at : at + size].astype(BF16) for h in range(2)], 0)

    def scalar(i):
        return jnp.concatenate([cols[h, :, i : i + 1] for h in range(2)], 0)

    hidden_ref[...] = whole(3 * LANES, hidden_ref.shape[1])
    d_up_ref[...] = whole(f_width + LANES, d_up_ref.shape[1])
    q, k, v = (whole(j * LANES, LANES) for j in range(3))
    d_att = whole(f_width, LANES)
    mean, inv = scalar(4), scalar(5)
    hot = one_hot(tokens, stats_ref.shape[1], 0)
    stats_ref[...] = jnp.concatenate([to_row(mean, hot), to_row(inv, hot)], 0)

    scale = LANES ** (-0.5)
    scores = dot(q, k, NT) * scale
    probs = jnp.exp(scores - jnp.max(scores, -1, keepdims=True))
    probs = probs / jnp.sum(probs, -1, keepdims=True)
    low = probs.astype(BF16)
    attended = dot(low, v, NN).astype(BF16)
    att_ref[...] = attended
    branch = dot(attended, wa_ref[...], NN) + dot(hidden_ref[...], wd_ref[...], NN)
    both[0, :, 0:width] = branch[0:half]
    both[1, :, 0:width] = branch[half:]
    d_probs = dot(d_att, v, NT)
    delta = jnp.sum(probs * d_probs, -1, keepdims=True)
    d_scores = (probs * (d_probs - delta)).astype(BF16)
    d_qn = dot(d_scores, k, NN) * scale
    d_kn = dot(d_scores, q, TN) * scale
    d_v = dot(low, d_att, TN).astype(BF16)

    def back(rows_low, i, g, d_rows):
        rstd, average = scalar(i), scalar(i + 2)
        unit = rows_low.astype(F32) / g
        d_unit = d_rows * g
        d_values = (
            d_unit
            - jnp.mean(d_unit, -1, keepdims=True)
            - unit * jnp.mean(d_unit * unit, -1, keepdims=True)
        ) * rstd
        return d_values.astype(BF16), jnp.sum(d_rows * unit, 0, keepdims=True), unit / rstd + average

    d_q, g_q, query = back(q, 0, qk_gain_ref[0:1], d_qn)
    d_k, g_k, key = back(k, 1, qk_gain_ref[1:2], d_kn)
    d_gain_ref[0:1, :] = g_q
    d_gain_ref[1:2, :] = g_k
    d_qkv_ref[:, tile(0)] = d_q
    d_qkv_ref[:, tile(1)] = d_k
    d_qkv_ref[:, tile(2)] = d_v
    d_normed = dot(d_qkv_ref[...], wq_ref[...], NT) + dot(d_up_ref[...], wu_ref[...], NT)
    both[0, :, width : 2 * width] = d_normed[0:half]
    both[1, :, width : 2 * width] = d_normed[half:]
    d_qf, d_kf, d_vf = d_q.astype(F32), d_k.astype(F32), d_v.astype(F32)
    t_1 = scalar(6)
    t_1 += jnp.sum(d_qf * c_ref[0:1] + d_kf * c_ref[1:2] + d_vf * c_ref[2:3], 1, keepdims=True)
    t_2 = scalar(7)
    t_2 += jnp.sum(d_qf * query + d_kf * key + d_vf * v.astype(F32), 1, keepdims=True)
    xhat = (x_ref[...].astype(F32) - mean) * inv
    normed_ref[...] = (xhat * gain_ref[...]).astype(BF16)
    part = jnp.sum(d_normed * xhat, 0, keepdims=True)
    n_col = send_ref.shape[0]
    rows_c = tokens // n_col
    lane = lax.broadcasted_iota(jnp.int32, (tokens, LANES), 1)
    place = lax.rem(lax.broadcasted_iota(jnp.int32, (tokens, LANES), 0), rows_c)
    ts = jnp.where(lane == place, t_1, 0.0) + jnp.where(lane == place + 32, t_2, 0.0)
    cols[0] = ts[0:half]
    cols[1] = ts[half:]

    w_tiles = width // LANES
    used = 2 * w_tiles * rows_c
    part = jnp.concatenate([part[:, tile(j)] for j in range(w_tiles)], 0)
    for c in range(n_col):
        h, at = divmod(c * rows_c, half)
        at = slice(at, at + rows_c)
        for j in range(2 * w_tiles):
            block[c, j * rows_c : (j + 1) * rows_c, :] = both[h, at, tile(j)]
        t_row = jnp.sum(cols[h, at, :], 0, keepdims=True)
        block[c, used : used + w_tiles + 1, :] = jnp.concatenate([part, t_row], 0)
    send_ref[...] = block[...].astype(BF16)


def finish_kernel(
    model_width, got_ref, stats_ref, x_ref, cot_ref, gain_ref, d_qk_ref,
    out_ref, grad_ref, d_gain_ref, d_qk_out, tot
):
    d_qk_out[...] = d_qk_ref[...]
    sum_blocks(got_ref, tot)
    rows, width = x_ref.shape
    tiles = width // LANES
    last = 2 * rows * tiles
    t_row = tot[last + tiles : last + tiles + 1, :]
    t_1 = to_column(t_row, one_hot(rows, LANES, 0))
    t_2 = to_column(t_row, one_hot(rows, LANES, 32))
    col = lax.axis_index("x") * lax.axis_size("y") + lax.axis_index("y")
    hot = one_hot(rows, stats_ref.shape[1], col * rows)
    mean, inv = to_column(stats_ref[0:1], hot), to_column(stats_ref[1:2], hot)
    for j in range(tiles):
        d_gain_ref[:, tile(j)] = tot[last + j : last + j + 1, :]
        x = x_ref[:, tile(j)].astype(F32)
        out_ref[:, tile(j)] = (x + tot[j * rows : (j + 1) * rows, :]).astype(BF16)
        xhat = (x - mean) * inv
        d_xhat = tot[(tiles + j) * rows : (tiles + j + 1) * rows, :] * gain_ref[:, tile(j)]
        grad = (d_xhat - t_1 / model_width - xhat * t_2 / model_width) * inv
        grad_ref[:, tile(j)] = (cot_ref[:, tile(j)].astype(F32) + grad).astype(BF16)


def shards(tokens_in, gain, w_qkv, qk_gain, w_up, w_attn_out, w_down, cotangent):
    rows_c, width = tokens_in.shape
    n_col = lax.axis_size(COL)
    n_z = lax.axis_size("z")
    tokens = rows_c * n_col
    rows = tokens // (2 * n_z)
    model_width = width * lax.axis_size(ROW)
    swap = [(0, 1), (1, 0)]
    hidden_w = w_up.shape[1]
    gain_row = gain.reshape(1, width)
    w_qkv2 = w_qkv.reshape(width, 3 * LANES)
    in_w, out_w = 3 * LANES + hidden_w, LANES + hidden_w
    tiles = (in_w + out_w) // LANES
    f_sum = in_w // LANES * (rows + 1) + 3
    sum_rows = f_sum + -(-out_w // LANES * rows // 16) * 16
    row_rows = tiles * rows + 8
    col_rows = 2 * width // LANES * rows_c + width // LANES + 1

    def scratch(*dims):
        return pltpu.VMEM(dims, F32)

    (sent,) = pl.pallas_call(
        spread_kernel,
        out_shape=[shape((n_col, col_rows, LANES))],
        in_specs=[pl.BlockSpec(memory_space=pl.ANY)] * 2,
        out_specs=[pl.BlockSpec(memory_space=pltpu.VMEM)],
        scratch_shapes=[
            pltpu.VMEM((rows_c, width), BF16),
            pltpu.VMEM((rows_c, width), BF16),
            scratch(col_rows, LANES),
            pltpu.SemaphoreType.DMA((2,)),
        ],
    )(tokens_in, cotangent)
    got = lax.all_to_all(sent, COL, 0, 0)

    own, other, x_all, cot_all = call(
        product_kernel,
        [
            shape((n_z, sum_rows, LANES), F32),
            shape((n_z, sum_rows, LANES)),
            shape((tokens, width)),
            shape((tokens, width)),
        ],
        [
            scratch(tokens + 8, width),
            scratch(tokens, width),
            scratch(tokens + 8, in_w),
            scratch(tokens, out_w),
            scratch(tokens, LANES),
            scratch(2, n_z, sum_rows, LANES),
        ],
        got,
        gain_row,
        w_qkv2,
        w_up,
        w_attn_out,
        w_down,
    )
    (half,) = call(
        lambda *refs: add_kernel(f_sum, *refs),
        [shape((n_z, sum_rows, LANES))],
        [scratch(sum_rows, LANES)],
        own,
        lax.ppermute(other, "core", swap),
    )
    got = lax.all_to_all(half, "z", 0, 0)

    sent, c_vec = call(
        lambda *refs: row_kernel(model_width, rows, f_sum, *refs),
        [shape((n_z, row_rows, LANES)), shape((16, LANES), F32)],
        [scratch(sum_rows, LANES), scratch(row_rows, LANES)],
        got,
        qk_gain,
    )
    mine = lax.all_to_all(sent, "z", 0, 0)
    theirs = lax.ppermute(mine, "core", swap)

    sent, d_qk_gain, attended, hidden, d_qkv, d_up, normed, stats = call(
        lambda *refs: attention_kernel(rows, *refs),
        [
            shape((n_col, col_rows, LANES)),
            shape((2, LANES), F32),
            shape((tokens, LANES)),
            shape((tokens, hidden_w)),
            shape((tokens, 3 * LANES)),
            shape((tokens, hidden_w)),
            shape((tokens, width)),
            shape((2, width), F32),
        ],
        [
            scratch(2, tokens // 2, in_w + out_w),
            scratch(2, tokens // 2, LANES),
            scratch(n_col, col_rows, LANES),
        ],
        mine,
        theirs,
        c_vec,
        x_all,
        gain_row,
        qk_gain,
        w_qkv2,
        w_up,
        w_attn_out,
        w_down,
    )
    got = lax.all_to_all(sent, COL, 0, 0)
    d_w_attn_out = dot(attended, cot_all, TN).astype(BF16)
    d_w_down = dot(hidden, cot_all, TN).astype(BF16)
    d_w_qkv = dot(normed, d_qkv, TN).astype(BF16).reshape(w_qkv.shape)
    d_w_up = dot(normed, d_up, TN).astype(BF16)
    layer_out, token_grad, d_gain, d_qk_gain = call(
        lambda *refs: finish_kernel(model_width, *refs),
        [
            shape((rows_c, width)),
            shape((rows_c, width)),
            shape((1, width), F32),
            shape((2, LANES), F32),
        ],
        [scratch(col_rows, LANES)],
        got,
        stats,
        tokens_in,
        cotangent,
        gain_row,
        d_qk_gain,
    )
    return (
        layer_out,
        token_grad,
        d_gain.reshape(width),
        d_w_qkv,
        d_qk_gain,
        d_w_up,
        d_w_attn_out,
        d_w_down,
    )


def solution(mesh):
    fine = Mesh(mesh.devices.reshape(-1, 2, 4, 8), ("z", "core", "x", "y"))
    in_specs = (
        P(COL, ROW),
        P(ROW),
        P(ROW, None, COL),
        P(None, COL),
        P(ROW, COL),
        P(COL, ROW),
        P(COL, ROW),
        P(COL, ROW),
    )
    out_specs = (
        P(COL, ROW),
        P(COL, ROW),
        P(ROW),
        P(ROW, None, COL),
        P(None, COL),
        P(ROW, COL),
        P(COL, ROW),
        P(COL, ROW),
    )
    return jax.shard_map(shards, mesh=fine, in_specs=in_specs, out_specs=out_specs, check_vma=False)
```

```python
import jax
import jax.numpy as jnp
from jax import lax
from jax.experimental import pallas as pl
from jax.experimental.pallas import tpu as pltpu
from jax.sharding import Mesh
from jax.sharding import PartitionSpec as P

LANES = 128
EPS = 1e-06
ROW = ("z", "core")
COL = ("x", "y")
F32 = jnp.float32
BF16 = jnp.bfloat16

NN = (((1,), (0,)), ((), ()))
NT = (((1,), (1,)), ((), ()))
TN = (((0,), (0,)), ((), ()))


def dot(a, b, dims):
    return lax.dot_general(a, b, dims, preferred_element_type=F32)


def split(values, parts):
    out = []
    for _ in range(parts):
        high = values.astype(BF16).astype(F32)
        out.append(high)
        values = values - high
    return out


def one_hot(rows, lanes, first):
    lane = lax.broadcasted_iota(jnp.int32, (rows, lanes), 1)
    return lane == lax.broadcasted_iota(jnp.int32, (rows, lanes), 0) + first


def to_column(row, hot):
    return jnp.sum(jnp.where(hot, row, 0.0), 1, keepdims=True)


def to_row(column, hot):
    return jnp.sum(jnp.where(hot, column, 0.0), 0, keepdims=True)


def two_to_row(a, b, rows):
    out = jnp.zeros((1, LANES), F32)
    for at, part in zip((0, 32, 64, 96), split(a, 2) + split(b, 2)):
        out = out + to_row(part, one_hot(rows, LANES, at))
    return out


def two_to_columns(row, rows):
    first = one_hot(rows, LANES, 0) | one_hot(rows, LANES, 32)
    second = one_hot(rows, LANES, 64) | one_hot(rows, LANES, 96)
    return to_column(row, first), to_column(row, second)


def tile(j):
    return slice(j * LANES, (j + 1) * LANES)


def call(kernel, outs, scratch, *args):
    return pl.pallas_call(
        kernel,
        out_shape=outs,
        in_specs=[pl.BlockSpec(memory_space=pltpu.VMEM)] * len(args),
        out_specs=[pl.BlockSpec(memory_space=pltpu.VMEM)] * len(outs),
        scratch_shapes=scratch,
        compiler_params=pltpu.CompilerParams(vmem_limit_bytes=16 * 2**20),
    )(*args)


def shape(dims, dtype=BF16):
    return jax.ShapeDtypeStruct(dims, dtype)


def spread_kernel(x_hbm, cot_hbm, out_ref, x_ref, cot_ref, block, sems):
    copies = [
        pltpu.make_async_copy(x_hbm, x_ref, sems.at[0]),
        pltpu.make_async_copy(cot_hbm, cot_ref, sems.at[1]),
    ]
    for copy in copies:
        copy.start()
    block[...] = jnp.zeros_like(block)
    rows, width = x_ref.shape
    at = 0
    for copy, ref in zip(copies, (x_ref, cot_ref)):
        copy.wait()
        values = ref[...].astype(F32)
        for j in range(width // LANES):
            block[at : at + rows, :] = values[:, tile(j)]
            at += rows
    out_ref[...] = jnp.broadcast_to(block[...].astype(BF16)[None], out_ref.shape)


def gather_kernel(got_ref, x_ref, cot_ref, xs, cs):
    n_col, width = got_ref.shape[0], x_ref.shape[1]
    rows = x_ref.shape[0] // n_col
    tiles = width // LANES
    for c in range(n_col):
        values = got_ref[c].astype(F32)
        here = slice(c * rows, (c + 1) * rows)
        for j in range(tiles):
            xs[here, tile(j)] = values[j * rows : (j + 1) * rows]
            cs[here, tile(j)] = values[(tiles + j) * rows : (tiles + j + 1) * rows]
    x_ref[...] = xs[...].astype(BF16)
    cot_ref[...] = cs[...].astype(BF16)


def products(
    which, rows, x_ref, cot_ref, gain_ref, wq_ref, wu_ref, wa_ref, wd_ref, out_ref, ps, fs, gs, st, lay
):
    width = x_ref.shape[1]
    n_z = out_ref.shape[0]
    half = n_z * rows
    mine = pl.ds(pl.multiple_of(which * half, 16), half)
    x = x_ref[mine, :].astype(F32)
    cot = cot_ref[mine, :]
    f_tiles, b_tiles = ps.shape[1] // LANES, gs.shape[1] // LANES
    f_sum = f_tiles * (rows + 1) + 3
    gain = gain_ref[...].reshape(1, width)
    gains = jnp.concatenate(split(gain, 3) + [jnp.zeros((5, width), F32)], 0)
    scaled = jnp.concatenate([x * gain, gains], 0)
    xg = scaled.astype(BF16)
    xg_low = (scaled - xg.astype(F32)).astype(BF16)
    fine = []
    for j in range(2):
        p = dot(xg, wq_ref[j], NN) + dot(xg_low, wq_ref[j], NN)
        ps[:, tile(j)] = p.astype(BF16).astype(F32)
        fs[:, tile(j)] = p - ps[:, tile(j)]
        fine.append(jnp.sum(p[half:], 0, keepdims=True))
    ps[:, tile(2)] = dot(xg, wq_ref[2], NN)
    ps[:, 3 * LANES :] = dot(xg, wu_ref[...], NN)
    gs[:, 0 : wa_ref.shape[0]] = dot(cot, wa_ref[...], NT)
    gs[:, wa_ref.shape[0] :] = dot(cot, wd_ref[...], NT)
    c_vec = jnp.sum(ps[half:, :], 0, keepdims=True)
    s_1 = jnp.sum(x, 1, keepdims=True)
    s_2 = jnp.sum(x * x, 1, keepdims=True)
    lane = lax.broadcasted_iota(jnp.int32, (half, LANES), 1)
    place = lax.rem(lax.broadcasted_iota(jnp.int32, (half, LANES), 0), rows)
    st[...] = jnp.where(lane == place, s_1, 0.0) + jnp.where(lane == place + 32, s_2, 0.0)
    c_rows = jnp.concatenate(fine + [c_vec[:, tile(j)] for j in range(2, f_tiles)], 0)
    c_rows, c_low = split(c_rows, 2)
    low_at = f_sum + b_tiles * rows
    fill = jnp.zeros((lay.shape[1] - low_at - 2 * rows - f_tiles, LANES), F32)
    c_low = jnp.concatenate([c_low, fill], 0)
    for d in range(n_z):
        at = slice(d * rows, (d + 1) * rows)
        for j in range(f_tiles):
            lay[d, j * rows : (j + 1) * rows, :] = ps[at, tile(j)]
        stat = jnp.sum(st[at, :], 0, keepdims=True)
        lay[d, f_tiles * rows : f_sum, :] = jnp.concatenate([c_rows] + split(stat, 3), 0)
        for j in range(b_tiles):
            lay[d, f_sum + j * rows : f_sum + (j + 1) * rows, :] = gs[at, tile(j)]
        for j in range(2):
            lay[d, low_at + j * rows : low_at + (j + 1) * rows, :] = fs[at, tile(j)]
        lay[d, low_at + 2 * rows :, :] = c_low
    out_ref[...] = lay[...].astype(out_ref.dtype)


def other_kernel(rows, got_ref, gain_ref, wq_ref, wu_ref, wa_ref, wd_ref, out_ref, x_ref, cot_ref, xs, cs, *scr):
    gather_kernel(got_ref, x_ref, cot_ref, xs, cs)
    other = 1 - lax.axis_index("core")
    products(other, rows, x_ref, cot_ref, gain_ref, wq_ref, wu_ref, wa_ref, wd_ref, out_ref, *scr)


def own_kernel(rows, x_ref, cot_ref, gain_ref, wq_ref, wu_ref, wa_ref, wd_ref, out_ref, *scr):
    core = lax.axis_index("core")
    products(core, rows, x_ref, cot_ref, gain_ref, wq_ref, wu_ref, wa_ref, wd_ref, out_ref, *scr)


def fine_pairs(rows, f_sum, low_at):
    tiles = f_sum // (rows + 1)
    c_at, c_low_at = tiles * rows, low_at + 2 * rows
    return (
        (slice(0, 2 * rows), slice(low_at, low_at + 2 * rows)),
        (slice(c_at, c_at + tiles), slice(c_low_at, c_low_at + tiles)),
    )


def add_kernel(rows, f_sum, low_at, own_ref, came_ref, out_ref, block):
    for d in range(own_ref.shape[0]):
        block[...] = own_ref[d] + came_ref[d].astype(F32)
        for high, low in fine_pairs(rows, f_sum, low_at):
            whole = block[high, :] + block[low, :]
            block[high, :] = whole.astype(BF16).astype(F32)
            block[low, :] = whole - block[high, :]
        stat = jnp.sum(block[f_sum - 3 : f_sum, :], 0, keepdims=True)
        block[f_sum - 3 : f_sum, :] = jnp.concatenate(split(stat, 3), 0)
        out_ref[d] = block[...].astype(BF16)


def gelu_parts(x):
    c = 0.7978845608028654
    t = jnp.tanh(c * (x + 0.044715 * (x * x * x)))
    half = 0.5 * (1.0 + t)
    slope = half + 0.5 * x * (1.0 - t * t) * (c * (1.0 + 3 * 0.044715 * (x * x)))
    return x * half, slope


def sum_blocks(got_ref, tot):
    total = got_ref[0].astype(F32)
    for d in range(1, got_ref.shape[0]):
        total = total + got_ref[d].astype(F32)
    tot[...] = total


def row_kernel(
    model_width, rows, f_sum, low_at, got_ref, qk_gain_ref, out_ref, c_ref, tot, block
):
    sum_blocks(got_ref, tot)
    for high, low in fine_pairs(rows, f_sum, low_at):
        tot[high, :] = tot[high, :] + tot[low, :]
    tiles = (f_sum - 3) // (rows + 1)
    c_ref[0:tiles, :] = tot[tiles * rows : tiles * rows + tiles, :]
    c_ref[tiles:, :] = jnp.zeros((c_ref.shape[0] - tiles, LANES), F32)
    stat = jnp.sum(tot[f_sum - 3 : f_sum, :], 0, keepdims=True)
    mean = to_column(stat, one_hot(rows, LANES, 0)) / model_width
    var = to_column(stat, one_hot(rows, LANES, 32)) / model_width - mean * mean
    inv = lax.rsqrt(var + EPS)

    def merged(j):
        return (tot[j * rows : (j + 1) * rows, :] - mean * c_ref[j : j + 1, :]) * inv

    def norm(j):
        values = merged(j)
        average = jnp.mean(values, -1, keepdims=True)
        centred = values - average
        rstd = lax.rsqrt(jnp.mean(centred * centred, -1, keepdims=True) + EPS)
        return centred * rstd * qk_gain_ref[j : j + 1], rstd, average

    block[0:rows, :], rstd_q, mean_q = norm(0)
    block[rows : 2 * rows, :], rstd_k, mean_k = norm(1)
    block[2 * rows : 3 * rows, :] = merged(2)
    back = tiles * rows
    block[back : back + rows, :] = tot[f_sum : f_sum + rows, :]
    s_1 = jnp.zeros((rows, LANES), F32)
    s_2 = jnp.zeros((rows, LANES), F32)
    for j in range(3, tiles):
        up = merged(j)
        hidden, slope = gelu_parts(up)
        block[j * rows : (j + 1) * rows, :] = hidden
        at = (j - 2) * rows
        d_hidden = tot[f_sum + at : f_sum + at + rows, :].astype(BF16).astype(F32)
        d_up = (d_hidden * slope).astype(BF16).astype(F32)
        block[back + at : back + at + rows, :] = d_up
        s_1 = s_1 + d_up * c_ref[j : j + 1, :]
        s_2 = s_2 + d_up * up
    s_1 = jnp.sum(s_1, 1, keepdims=True)
    s_2 = jnp.sum(s_2, 1, keepdims=True)
    last = (2 * tiles - 2) * rows
    pairs = ((rstd_q, rstd_k), (mean_q, mean_k), (mean, inv), (s_1, s_2))
    block[last:, :] = jnp.concatenate(
        [two_to_row(a, b, rows) for a, b in pairs]
        + [jnp.zeros((block.shape[0] - last - len(pairs), LANES), F32)],
        0,
    )
    out_ref[...] = jnp.broadcast_to(block[...].astype(BF16)[None], out_ref.shape)


def attention_kernel(
    rows, mine_ref, theirs_ref, c_ref, x_ref, gain_ref, qk_gain_ref, wq_ref, wu_ref, wa_ref, wd_ref,
    send_ref, d_gain_ref, att_ref, hidden_ref, d_qkv_ref, d_up_ref, normed_ref, stats_ref,
    both, cols, block
):
    n_z = mine_ref.shape[0]
    tokens, width = x_ref.shape
    half = tokens // 2
    core = lax.axis_index("core")
    tiles = both.shape[2] // LANES
    f_width = 3 * LANES + hidden_ref.shape[1]
    lane = lax.broadcasted_iota(jnp.int32, (rows, LANES), 1)
    for ref, h in ((mine_ref, core), (theirs_ref, 1 - core)):
        for d in range(n_z):
            values = ref[d].astype(F32)
            at = slice(d * rows, (d + 1) * rows)
            for j in range(tiles):
                both[h, at, tile(j)] = values[j * rows : (j + 1) * rows]
            scalars = jnp.zeros((rows, LANES), F32)
            for i in range(4):
                a, b = two_to_columns(values[tiles * rows + i : tiles * rows + i + 1], rows)
                scalars = jnp.where(lane == 2 * i, a, scalars)
                scalars = jnp.where(lane == 2 * i + 1, b, scalars)
            cols[h, at, :] = scalars

    def whole(at, size):
        return jnp.concatenate([both[h, :, at : at + size].astype(BF16) for h in range(2)], 0)

    def scalar(i):
        return jnp.concatenate([cols[h, :, i : i + 1] for h in range(2)], 0)

    hidden_ref[...] = whole(3 * LANES, hidden_ref.shape[1])
    d_up_ref[...] = whole(f_width + LANES, d_up_ref.shape[1])
    q, k, v = (whole(j * LANES, LANES) for j in range(3))
    d_att = whole(f_width, LANES)
    mean, inv = scalar(4), scalar(5)
    hot = one_hot(tokens, stats_ref.shape[1], 0)
    stats_ref[...] = jnp.concatenate([to_row(mean, hot), to_row(inv, hot)], 0)

    scale = LANES ** (-0.5)
    scores = dot(q, k, NT) * scale
    probs = jnp.exp(scores - jnp.max(scores, -1, keepdims=True))
    probs = probs / jnp.sum(probs, -1, keepdims=True)
    low = probs.astype(BF16)
    attended = dot(low, v, NN).astype(BF16)
    att_ref[...] = attended
    branch = dot(attended, wa_ref[...], NN) + dot(hidden_ref[...], wd_ref[...], NN)
    both[0, :, 0:width] = branch[0:half]
    both[1, :, 0:width] = branch[half:]
    d_probs = dot(d_att, v, NT)
    delta = jnp.sum(probs * d_probs, -1, keepdims=True)
    d_scores = (probs * (d_probs - delta)).astype(BF16)
    d_qn = dot(d_scores, k, NN) * scale
    d_kn = dot(d_scores, q, TN) * scale
    d_v = dot(low, d_att, TN).astype(BF16)

    def back(rows_low, i, g, d_rows):
        rstd, average = scalar(i), scalar(i + 2)
        unit = rows_low.astype(F32) / g
        d_unit = d_rows * g
        d_values = (
            d_unit
            - jnp.mean(d_unit, -1, keepdims=True)
            - unit * jnp.mean(d_unit * unit, -1, keepdims=True)
        ) * rstd
        return d_values.astype(BF16), jnp.sum(d_rows * unit, 0, keepdims=True), unit / rstd + average

    d_q, g_q, query = back(q, 0, qk_gain_ref[0:1], d_qn)
    d_k, g_k, key = back(k, 1, qk_gain_ref[1:2], d_kn)
    d_gain_ref[0:1, :] = g_q
    d_gain_ref[1:2, :] = g_k
    d_qkv_ref[:, tile(0)] = d_q
    d_qkv_ref[:, tile(1)] = d_k
    d_qkv_ref[:, tile(2)] = d_v
    d_normed = dot(d_up_ref[...], wu_ref[...], NT)
    for j, d_j in enumerate((d_q, d_k, d_v)):
        d_normed += dot(d_j, wq_ref[j], NT)
    both[0, :, width : 2 * width] = d_normed[0:half]
    both[1, :, width : 2 * width] = d_normed[half:]
    d_qf, d_kf, d_vf = d_q.astype(F32), d_k.astype(F32), d_v.astype(F32)
    t_1 = scalar(6)
    t_1 += jnp.sum(d_qf * c_ref[0:1] + d_kf * c_ref[1:2] + d_vf * c_ref[2:3], 1, keepdims=True)
    t_2 = scalar(7)
    t_2 += jnp.sum(d_qf * query + d_kf * key + d_vf * v.astype(F32), 1, keepdims=True)
    xhat = (x_ref[...].astype(F32) - mean) * inv
    normed_ref[...] = (xhat * gain_ref[...].reshape(1, width)).astype(BF16)
    part = jnp.sum(d_normed * xhat, 0, keepdims=True)
    n_col = send_ref.shape[0]
    rows_c = tokens // n_col
    lane = lax.broadcasted_iota(jnp.int32, (tokens, LANES), 1)
    place = lax.rem(lax.broadcasted_iota(jnp.int32, (tokens, LANES), 0), rows_c)
    ts = jnp.where(lane == place, t_1, 0.0) + jnp.where(lane == place + 32, t_2, 0.0)
    cols[0] = ts[0:half]
    cols[1] = ts[half:]

    w_tiles = width // LANES
    used = 2 * w_tiles * rows_c
    part = jnp.concatenate([part[:, tile(j)] for j in range(w_tiles)], 0)
    for c in range(n_col):
        h, at = divmod(c * rows_c, half)
        at = slice(at, at + rows_c)
        for j in range(2 * w_tiles):
            block[c, j * rows_c : (j + 1) * rows_c, :] = both[h, at, tile(j)]
        t_row = jnp.sum(cols[h, at, :], 0, keepdims=True)
        block[c, used : used + w_tiles + 1, :] = jnp.concatenate([part, t_row], 0)
    send_ref[...] = block[...].astype(BF16)


def finish_kernel(
    model_width, got_ref, stats_ref, x_ref, cot_ref, gain_ref, d_qk_ref,
    out_ref, grad_ref, d_gain_ref, d_qk_out, tot
):
    gain = gain_ref[...].reshape(1, x_ref.shape[1])
    d_qk_out[...] = d_qk_ref[...]
    sum_blocks(got_ref, tot)
    rows, width = x_ref.shape
    tiles = width // LANES
    last = 2 * rows * tiles
    t_row = tot[last + tiles : last + tiles + 1, :]
    t_1 = to_column(t_row, one_hot(rows, LANES, 0))
    t_2 = to_column(t_row, one_hot(rows, LANES, 32))
    col = lax.axis_index("x") * lax.axis_size("y") + lax.axis_index("y")
    hot = one_hot(rows, stats_ref.shape[1], col * rows)
    mean, inv = to_column(stats_ref[0:1], hot), to_column(stats_ref[1:2], hot)
    for j in range(tiles):
        d_gain_ref[tile(j)] = tot[last + j, :]
        x = x_ref[:, tile(j)].astype(F32)
        out_ref[:, tile(j)] = (x + tot[j * rows : (j + 1) * rows, :]).astype(BF16)
        xhat = (x - mean) * inv
        d_xhat = tot[(tiles + j) * rows : (tiles + j + 1) * rows, :] * gain[:, tile(j)]
        grad = (d_xhat - t_1 / model_width - xhat * t_2 / model_width) * inv
        grad_ref[:, tile(j)] = (cot_ref[:, tile(j)].astype(F32) + grad).astype(BF16)


def shards(tokens_in, gain, w_qkv, qk_gain, w_up, w_attn_out, w_down, cotangent):
    rows_c, width = tokens_in.shape
    n_col = lax.axis_size(COL)
    n_z = lax.axis_size("z")
    tokens = rows_c * n_col
    rows = tokens // (2 * n_z)
    model_width = width * lax.axis_size(ROW)
    swap = [(0, 1), (1, 0)]
    hidden_w = w_up.shape[1]
    w_qkv3 = jnp.transpose(w_qkv, (1, 0, 2))
    in_w, out_w = 3 * LANES + hidden_w, LANES + hidden_w
    tiles = (in_w + out_w) // LANES
    f_sum = in_w // LANES * (rows + 1) + 3
    low_at = f_sum + out_w // LANES * rows
    sum_rows = -(-(low_at + 2 * rows + in_w // LANES) // 16) * 16
    row_rows = tiles * rows + 8
    col_rows = 2 * width // LANES * rows_c + width // LANES + 1

    def scratch(*dims):
        return pltpu.VMEM(dims, F32)

    (sent,) = pl.pallas_call(
        spread_kernel,
        out_shape=[shape((n_col, col_rows, LANES))],
        in_specs=[pl.BlockSpec(memory_space=pltpu.HBM)] * 2,
        out_specs=[pl.BlockSpec(memory_space=pltpu.VMEM)],
        scratch_shapes=[
            pltpu.VMEM((rows_c, width), BF16),
            pltpu.VMEM((rows_c, width), BF16),
            scratch(col_rows, LANES),
            pltpu.SemaphoreType.DMA((2,)),
        ],
    )(tokens_in, cotangent)
    got = lax.all_to_all(sent, COL, 0, 0)

    weights = (gain, w_qkv3, w_up, w_attn_out, w_down)
    work = [
        scratch(tokens // 2 + 8, in_w),
        scratch(tokens // 2 + 8, 2 * LANES),
        scratch(tokens // 2, out_w),
        scratch(tokens // 2, LANES),
        scratch(n_z, sum_rows, LANES),
    ]
    other, x_all, cot_all = call(
        lambda *refs: other_kernel(rows, *refs),
        [shape((n_z, sum_rows, LANES)), shape((tokens, width)), shape((tokens, width))],
        [scratch(tokens, width), scratch(tokens, width)] + work,
        got,
        *weights,
    )
    (own,) = call(
        lambda *refs: own_kernel(rows, *refs),
        [shape((n_z, sum_rows, LANES), F32)],
        work,
        x_all,
        cot_all,
        *weights,
    )
    (half,) = call(
        lambda *refs: add_kernel(rows, f_sum, low_at, *refs),
        [shape((n_z, sum_rows, LANES))],
        [scratch(sum_rows, LANES)],
        own,
        lax.ppermute(other, "core", swap),
    )
    got = lax.all_to_all(half, "z", 0, 0)

    sent, c_vec = call(
        lambda *refs: row_kernel(model_width, rows, f_sum, low_at, *refs),
        [shape((n_z, row_rows, LANES)), shape((16, LANES), F32)],
        [scratch(sum_rows, LANES), scratch(row_rows, LANES)],
        got,
        qk_gain,
    )
    mine = lax.all_to_all(sent, "z", 0, 0)
    theirs = lax.ppermute(mine, "core", swap)

    sent, d_qk_gain, attended, hidden, d_qkv, d_up, normed, stats = call(
        lambda *refs: attention_kernel(rows, *refs),
        [
            shape((n_col, col_rows, LANES)),
            shape((2, LANES), F32),
            shape((tokens, LANES)),
            shape((tokens, hidden_w)),
            shape((tokens, 3 * LANES)),
            shape((tokens, hidden_w)),
            shape((tokens, width)),
            shape((2, width), F32),
        ],
        [
            scratch(2, tokens // 2, in_w + out_w),
            scratch(2, tokens // 2, LANES),
            scratch(n_col, col_rows, LANES),
        ],
        mine,
        theirs,
        c_vec,
        x_all,
        gain,
        qk_gain,
        w_qkv3,
        w_up,
        w_attn_out,
        w_down,
    )
    got = lax.all_to_all(sent, COL, 0, 0)
    d_w_attn_out = dot(attended, cot_all, TN).astype(BF16)
    d_w_down = dot(hidden, cot_all, TN).astype(BF16)
    d_w_qkv = dot(normed, d_qkv, TN).astype(BF16).reshape(w_qkv.shape)
    d_w_up = dot(normed, d_up, TN).astype(BF16)
    layer_out, token_grad, d_gain, d_qk_gain = call(
        lambda *refs: finish_kernel(model_width, *refs),
        [
            shape((rows_c, width)),
            shape((rows_c, width)),
            shape((width,), F32),
            shape((2, LANES), F32),
        ],
        [scratch(col_rows, LANES)],
        got,
        stats,
        tokens_in,
        cotangent,
        gain,
        d_qk_gain,
    )
    return (
        layer_out,
        token_grad,
        d_gain,
        d_w_qkv,
        d_qk_gain,
        d_w_up,
        d_w_attn_out,
        d_w_down,
    )


def solution(mesh):
    fine = Mesh(mesh.devices.reshape(-1, 2, 4, 8), ("z", "core", "x", "y"))
    in_specs = (
        P(COL, ROW),
        P(ROW),
        P(ROW, None, COL),
        P(None, COL),
        P(ROW, COL),
        P(COL, ROW),
        P(COL, ROW),
        P(COL, ROW),
    )
    out_specs = (
        P(COL, ROW),
        P(COL, ROW),
        P(ROW),
        P(ROW, None, COL),
        P(None, COL),
        P(ROW, COL),
        P(COL, ROW),
        P(COL, ROW),
    )
    return jax.shard_map(shards, mesh=fine, in_specs=in_specs, out_specs=out_specs, check_vma=False)
```

```python
import jax
import jax.numpy as jnp
from jax import lax
from jax.experimental import pallas as pl
from jax.experimental.pallas import tpu as pltpu
from jax.sharding import Mesh
from jax.sharding import PartitionSpec as P

LANES = 128
EPS = 1e-06
ROW = ("z", "core")
COL = ("x", "y")
F32 = jnp.float32
BF16 = jnp.bfloat16

NN = (((1,), (0,)), ((), ()))
NT = (((1,), (1,)), ((), ()))
TN = (((0,), (0,)), ((), ()))


def dot(a, b, dims):
    return lax.dot_general(a, b, dims, preferred_element_type=F32)


def split(values, parts):
    out = []
    for _ in range(parts):
        high = values.astype(BF16).astype(F32)
        out.append(high)
        values = values - high
    return out


def one_hot(rows, lanes, first):
    lane = lax.broadcasted_iota(jnp.int32, (rows, lanes), 1)
    return lane == lax.broadcasted_iota(jnp.int32, (rows, lanes), 0) + first


def to_column(row, hot):
    return jnp.sum(jnp.where(hot, row, 0.0), 1, keepdims=True)


def to_row(column, hot):
    return jnp.sum(jnp.where(hot, column, 0.0), 0, keepdims=True)


def two_to_row(a, b, rows):
    out = jnp.zeros((1, LANES), F32)
    for at, part in zip((0, 32, 64, 96), split(a, 2) + split(b, 2)):
        out = out + to_row(part, one_hot(rows, LANES, at))
    return out


def two_to_columns(row, rows):
    first = one_hot(rows, LANES, 0) | one_hot(rows, LANES, 32)
    second = one_hot(rows, LANES, 64) | one_hot(rows, LANES, 96)
    return to_column(row, first), to_column(row, second)


def tile(j):
    return slice(j * LANES, (j + 1) * LANES)


def call(kernel, outs, scratch, *args):
    return pl.pallas_call(
        kernel,
        out_shape=outs,
        in_specs=[pl.BlockSpec(memory_space=pltpu.VMEM)] * len(args),
        out_specs=[pl.BlockSpec(memory_space=pltpu.VMEM)] * len(outs),
        scratch_shapes=scratch,
        compiler_params=pltpu.CompilerParams(vmem_limit_bytes=16 * 2**20),
    )(*args)


def shape(dims, dtype=BF16):
    return jax.ShapeDtypeStruct(dims, dtype)


def spread_kernel(x_hbm, cot_hbm, out_ref, x_ref, cot_ref, block, sems):
    copies = [
        pltpu.make_async_copy(x_hbm, x_ref, sems.at[0]),
        pltpu.make_async_copy(cot_hbm, cot_ref, sems.at[1]),
    ]
    for copy in copies:
        copy.start()
    block[...] = jnp.zeros_like(block)
    rows, width = x_ref.shape
    at = 0
    for copy, ref in zip(copies, (x_ref, cot_ref)):
        copy.wait()
        values = ref[...].astype(F32)
        for j in range(width // LANES):
            block[at : at + rows, :] = values[:, tile(j)]
            at += rows
    out_ref[...] = jnp.broadcast_to(block[...].astype(BF16)[None], out_ref.shape)


def gather_kernel(got_ref, x_ref, cot_ref, xs, cs):
    n_col, width = got_ref.shape[0], x_ref.shape[1]
    rows = x_ref.shape[0] // n_col
    tiles = width // LANES
    for c in range(n_col):
        values = got_ref[c].astype(F32)
        here = slice(c * rows, (c + 1) * rows)
        for j in range(tiles):
            xs[here, tile(j)] = values[j * rows : (j + 1) * rows]
            cs[here, tile(j)] = values[(tiles + j) * rows : (tiles + j + 1) * rows]
    x_ref[...] = xs[...].astype(BF16)
    cot_ref[...] = cs[...].astype(BF16)


def products(
    which, rows, x_ref, cot_ref, gain_ref, wq_ref, wu_ref, wa_ref, wd_ref, out_ref, ps, fs, gs, st, lay
):
    width = x_ref.shape[1]
    n_z = out_ref.shape[0]
    half = n_z * rows
    mine = pl.ds(pl.multiple_of(which * half, 16), half)
    x = x_ref[mine, :].astype(F32)
    cot = cot_ref[mine, :]
    f_tiles, b_tiles = ps.shape[1] // LANES, gs.shape[1] // LANES
    f_sum = f_tiles * (rows + 1) + 3
    gain = gain_ref[...].reshape(1, width)
    gains = jnp.concatenate(split(gain, 3) + [jnp.zeros((5, width), F32)], 0)
    scaled = jnp.concatenate([x * gain, gains], 0)
    xg = scaled.astype(BF16)
    xg_low = (scaled - xg.astype(F32)).astype(BF16)
    fine = []
    for j in range(2):
        p = dot(xg, wq_ref[j], NN) + dot(xg_low, wq_ref[j], NN)
        ps[:, tile(j)] = p.astype(BF16).astype(F32)
        fs[:, tile(j)] = p - ps[:, tile(j)]
        fine.append(jnp.sum(p[half:], 0, keepdims=True))
    ps[:, tile(2)] = dot(xg, wq_ref[2], NN)
    ps[:, 3 * LANES :] = dot(xg, wu_ref[...], NN)
    gs[:, 0 : wa_ref.shape[0]] = dot(cot, wa_ref[...], NT)
    gs[:, wa_ref.shape[0] :] = dot(cot, wd_ref[...], NT)
    c_vec = jnp.sum(ps[half:, :], 0, keepdims=True)
    s_1 = jnp.sum(x, 1, keepdims=True)
    s_2 = jnp.sum(x * x, 1, keepdims=True)
    lane = lax.broadcasted_iota(jnp.int32, (half, LANES), 1)
    place = lax.rem(lax.broadcasted_iota(jnp.int32, (half, LANES), 0), rows)
    st[...] = jnp.where(lane == place, s_1, 0.0) + jnp.where(lane == place + 32, s_2, 0.0)
    c_rows = jnp.concatenate(fine + [c_vec[:, tile(j)] for j in range(2, f_tiles)], 0)
    c_rows, c_low = split(c_rows, 2)
    low_at = f_sum + b_tiles * rows
    fill = jnp.zeros((lay.shape[1] - low_at - 2 * rows - f_tiles, LANES), F32)
    c_low = jnp.concatenate([c_low, fill], 0)
    for d in range(n_z):
        at = slice(d * rows, (d + 1) * rows)
        for j in range(f_tiles):
            lay[d, j * rows : (j + 1) * rows, :] = ps[at, tile(j)]
        stat = jnp.sum(st[at, :], 0, keepdims=True)
        lay[d, f_tiles * rows : f_sum, :] = jnp.concatenate([c_rows] + split(stat, 3), 0)
        for j in range(b_tiles):
            lay[d, f_sum + j * rows : f_sum + (j + 1) * rows, :] = gs[at, tile(j)]
        for j in range(2):
            lay[d, low_at + j * rows : low_at + (j + 1) * rows, :] = fs[at, tile(j)]
        lay[d, low_at + 2 * rows :, :] = c_low
    out_ref[...] = lay[...].astype(out_ref.dtype)


def other_kernel(rows, got_ref, gain_ref, wq_ref, wu_ref, wa_ref, wd_ref, out_ref, x_ref, cot_ref, xs, cs, *scr):
    gather_kernel(got_ref, x_ref, cot_ref, xs, cs)
    other = 1 - lax.axis_index("core")
    products(other, rows, x_ref, cot_ref, gain_ref, wq_ref, wu_ref, wa_ref, wd_ref, out_ref, *scr)


def own_kernel(rows, x_ref, cot_ref, gain_ref, wq_ref, wu_ref, wa_ref, wd_ref, out_ref, *scr):
    core = lax.axis_index("core")
    products(core, rows, x_ref, cot_ref, gain_ref, wq_ref, wu_ref, wa_ref, wd_ref, out_ref, *scr)


def fine_pairs(rows, f_sum, low_at):
    tiles = f_sum // (rows + 1)
    c_at, c_low_at = tiles * rows, low_at + 2 * rows
    return (
        (slice(0, 2 * rows), slice(low_at, low_at + 2 * rows)),
        (slice(c_at, c_at + tiles), slice(c_low_at, c_low_at + tiles)),
    )


def add_kernel(rows, f_sum, low_at, own_ref, came_ref, out_ref, block):
    for d in range(own_ref.shape[0]):
        block[...] = own_ref[d] + came_ref[d].astype(F32)
        for high, low in fine_pairs(rows, f_sum, low_at):
            whole = block[high, :] + block[low, :]
            block[high, :] = whole.astype(BF16).astype(F32)
            block[low, :] = whole - block[high, :]
        stat = jnp.sum(block[f_sum - 3 : f_sum, :], 0, keepdims=True)
        block[f_sum - 3 : f_sum, :] = jnp.concatenate(split(stat, 3), 0)
        out_ref[d] = block[...].astype(BF16)


def gelu_parts(x):
    c = 0.7978845608028654
    t = jnp.tanh(c * (x + 0.044715 * (x * x * x)))
    half = 0.5 * (1.0 + t)
    slope = half + 0.5 * x * (1.0 - t * t) * (c * (1.0 + 3 * 0.044715 * (x * x)))
    return x * half, slope


def sum_blocks(got_ref, tot):
    total = got_ref[0].astype(F32)
    for d in range(1, got_ref.shape[0]):
        total = total + got_ref[d].astype(F32)
    tot[...] = total


def row_kernel(
    model_width, rows, f_sum, low_at, got_ref, qk_gain_ref, out_ref, c_ref, tot, block
):
    sum_blocks(got_ref, tot)
    for high, low in fine_pairs(rows, f_sum, low_at):
        tot[high, :] = tot[high, :] + tot[low, :]
    tiles = (f_sum - 3) // (rows + 1)
    c_ref[0:tiles, :] = tot[tiles * rows : tiles * rows + tiles, :]
    c_ref[tiles:, :] = jnp.zeros((c_ref.shape[0] - tiles, LANES), F32)
    stat = jnp.sum(tot[f_sum - 3 : f_sum, :], 0, keepdims=True)
    mean = to_column(stat, one_hot(rows, LANES, 0)) / model_width
    var = to_column(stat, one_hot(rows, LANES, 32)) / model_width - mean * mean
    inv = lax.rsqrt(var + EPS)

    def merged(j):
        return (tot[j * rows : (j + 1) * rows, :] - mean * c_ref[j : j + 1, :]) * inv

    def norm(j):
        values = merged(j)
        average = jnp.mean(values, -1, keepdims=True)
        centred = values - average
        rstd = lax.rsqrt(jnp.mean(centred * centred, -1, keepdims=True) + EPS)
        return centred * rstd * qk_gain_ref[j : j + 1], rstd, average

    block[0:rows, :], rstd_q, mean_q = norm(0)
    block[rows : 2 * rows, :], rstd_k, mean_k = norm(1)
    block[2 * rows : 3 * rows, :] = merged(2)
    back = tiles * rows
    block[back : back + rows, :] = tot[f_sum : f_sum + rows, :]
    s_1 = jnp.zeros((rows, LANES), F32)
    s_2 = jnp.zeros((rows, LANES), F32)
    for j in range(3, tiles):
        up = merged(j)
        hidden, slope = gelu_parts(up)
        block[j * rows : (j + 1) * rows, :] = hidden
        at = (j - 2) * rows
        d_hidden = tot[f_sum + at : f_sum + at + rows, :].astype(BF16).astype(F32)
        d_up = (d_hidden * slope).astype(BF16).astype(F32)
        block[back + at : back + at + rows, :] = d_up
        s_1 = s_1 + d_up * c_ref[j : j + 1, :]
        s_2 = s_2 + d_up * up
    s_1 = jnp.sum(s_1, 1, keepdims=True)
    s_2 = jnp.sum(s_2, 1, keepdims=True)
    last = (2 * tiles - 2) * rows
    pairs = ((rstd_q, rstd_k), (mean_q, mean_k), (mean, inv), (s_1, s_2))
    block[last:, :] = jnp.concatenate(
        [two_to_row(a, b, rows) for a, b in pairs]
        + [jnp.zeros((block.shape[0] - last - len(pairs), LANES), F32)],
        0,
    )
    out_ref[...] = jnp.broadcast_to(block[...].astype(BF16)[None], out_ref.shape)


def unpack(rows, ref, half, cols):
    tiles = half.shape[-1] // LANES
    lane = lax.broadcasted_iota(jnp.int32, (rows, LANES), 1)
    for d in range(ref.shape[0]):
        values = ref[d].astype(F32)
        at = slice(d * rows, (d + 1) * rows)
        for j in range(tiles):
            half[at, tile(j)] = values[j * rows : (j + 1) * rows]
        scalars = jnp.zeros((rows, LANES), F32)
        for i in range(4):
            a, b = two_to_columns(values[tiles * rows + i : tiles * rows + i + 1], rows)
            scalars = jnp.where(lane == 2 * i, a, scalars)
            scalars = jnp.where(lane == 2 * i + 1, b, scalars)
        cols[at, :] = scalars


def mlp_products(values, wd_ref, wu_ref, part_ref, at):
    hidden_w, width = wd_ref.shape
    f_width = 3 * LANES + hidden_w
    part_ref[at, 0:width] = dot(values[:, 3 * LANES : f_width], wd_ref[...], NN)
    part_ref[at, width:] = dot(values[:, f_width + LANES :], wu_ref[...], NT)


def unpack_kernel(rows, mine_ref, wd_ref, wu_ref, out_ref, cols_ref, part_ref, half):
    unpack(rows, mine_ref, half, cols_ref)
    out_ref[...] = half[...].astype(BF16)
    mlp_products(out_ref[...], wd_ref, wu_ref, part_ref, slice(None))


def attention_kernel(
    rows, half_ref, half_cols_ref, half_part_ref, theirs_ref, c_ref, x_ref, gain_ref, qk_gain_ref, wq_ref, wu_ref, wa_ref, wd_ref,
    send_ref, d_gain_ref, att_ref, hidden_ref, d_qkv_ref, d_up_ref, normed_ref, stats_ref,
    full, wide, block, cols, cols_ref, mlp
):
    tokens, width = x_ref.shape
    half = tokens // 2
    core = lax.axis_index("core")
    f_width = 3 * LANES + hidden_ref.shape[1]
    unpack(rows, theirs_ref, wide, cols)
    for h, values, scalars in ((core, half_ref, half_cols_ref), (1 - core, wide, cols)):
        at = pl.ds(pl.multiple_of(h * half, 16), half)
        full[at, :] = values[...].astype(BF16)
        cols_ref[at, :] = scalars[...]
    mlp[pl.ds(pl.multiple_of(core * half, 16), half), :] = half_part_ref[...]
    other = pl.ds(pl.multiple_of((1 - core) * half, 16), half)
    mlp_products(wide[...].astype(BF16), wd_ref, wu_ref, mlp, other)

    def whole(at, size):
        return full[:, at : at + size]

    def scalar(i):
        return cols_ref[:, i : i + 1]

    hidden_ref[...] = whole(3 * LANES, hidden_ref.shape[1])
    d_up_ref[...] = whole(f_width + LANES, d_up_ref.shape[1])
    q, k, v = (whole(j * LANES, LANES) for j in range(3))
    d_att = whole(f_width, LANES)
    mean, inv = scalar(4), scalar(5)
    hot = one_hot(tokens, stats_ref.shape[1], 0)
    stats_ref[...] = jnp.concatenate([to_row(mean, hot), to_row(inv, hot)], 0)

    scale = LANES ** (-0.5)
    scores = dot(q, k, NT) * scale
    probs = jnp.exp(scores - jnp.max(scores, -1, keepdims=True))
    probs = probs / jnp.sum(probs, -1, keepdims=True)
    low = probs.astype(BF16)
    attended = dot(low, v, NN).astype(BF16)
    att_ref[...] = attended
    branch = dot(attended, wa_ref[...], NN) + mlp[:, 0:width]
    wide[:, 0:width] = branch[0:half]
    wide[:, width : 2 * width] = branch[half:]
    d_probs = dot(d_att, v, NT)
    delta = jnp.sum(probs * d_probs, -1, keepdims=True)
    d_scores = (probs * (d_probs - delta)).astype(BF16)
    d_qn = dot(d_scores, k, NN) * scale
    d_kn = dot(d_scores, q, TN) * scale
    d_v = dot(low, d_att, TN).astype(BF16)

    def back(rows_low, i, g, d_rows):
        rstd, average = scalar(i), scalar(i + 2)
        unit = rows_low.astype(F32) / g
        d_unit = d_rows * g
        d_values = (
            d_unit
            - jnp.mean(d_unit, -1, keepdims=True)
            - unit * jnp.mean(d_unit * unit, -1, keepdims=True)
        ) * rstd
        return d_values.astype(BF16), jnp.sum(d_rows * unit, 0, keepdims=True), unit / rstd + average

    d_q, g_q, query = back(q, 0, qk_gain_ref[0:1], d_qn)
    d_k, g_k, key = back(k, 1, qk_gain_ref[1:2], d_kn)
    d_gain_ref[0:1, :] = g_q
    d_gain_ref[1:2, :] = g_k
    d_qkv_ref[:, tile(0)] = d_q
    d_qkv_ref[:, tile(1)] = d_k
    d_qkv_ref[:, tile(2)] = d_v
    d_normed = mlp[:, width:]
    for j, d_j in enumerate((d_q, d_k, d_v)):
        d_normed += dot(d_j, wq_ref[j], NT)
    wide[:, 2 * width : 3 * width] = d_normed[0:half]
    wide[:, 3 * width : 4 * width] = d_normed[half:]
    d_qf, d_kf, d_vf = d_q.astype(F32), d_k.astype(F32), d_v.astype(F32)
    t_1 = scalar(6)
    t_1 += jnp.sum(d_qf * c_ref[0:1] + d_kf * c_ref[1:2] + d_vf * c_ref[2:3], 1, keepdims=True)
    t_2 = scalar(7)
    t_2 += jnp.sum(d_qf * query + d_kf * key + d_vf * v.astype(F32), 1, keepdims=True)
    xhat = (x_ref[...].astype(F32) - mean) * inv
    normed_ref[...] = (xhat * gain_ref[...].reshape(1, width)).astype(BF16)
    part = jnp.sum(d_normed * xhat, 0, keepdims=True)
    n_col = send_ref.shape[0]
    rows_c = tokens // n_col
    lane = lax.broadcasted_iota(jnp.int32, (tokens, LANES), 1)
    place = lax.rem(lax.broadcasted_iota(jnp.int32, (tokens, LANES), 0), rows_c)
    ts = jnp.where(lane == place, t_1, 0.0) + jnp.where(lane == place + 32, t_2, 0.0)
    cols[...] = ts[0:half] + pltpu.roll(ts[half:], 64, 1)

    w_tiles = width // LANES
    used = 2 * w_tiles * rows_c
    part = jnp.concatenate([part[:, tile(j)] for j in range(w_tiles)], 0)
    for c in range(n_col):
        h, at = divmod(c * rows_c, half)
        at = slice(at, at + rows_c)
        for i in range(2):
            for j in range(w_tiles):
                to = (i * w_tiles + j) * rows_c
                block[c, to : to + rows_c, :] = wide[at, tile((2 * i + h) * w_tiles + j)]
        t_row = jnp.sum(cols[at, :], 0, keepdims=True)
        block[c, used : used + w_tiles + 1, :] = jnp.concatenate([part, t_row], 0)
    send_ref[...] = block[...].astype(BF16)


def finish_kernel(
    model_width, got_ref, stats_ref, x_ref, cot_ref, gain_ref, d_qk_ref,
    out_ref, grad_ref, d_gain_ref, d_qk_out, tot
):
    gain = gain_ref[...].reshape(1, x_ref.shape[1])
    d_qk_out[...] = d_qk_ref[...]
    sum_blocks(got_ref, tot)
    rows, width = x_ref.shape
    tiles = width // LANES
    last = 2 * rows * tiles
    t_row = tot[last + tiles : last + tiles + 1, :]
    col = lax.axis_index("x") * lax.axis_size("y") + lax.axis_index("y")
    upper = jnp.where(col * 2 >= lax.axis_size("x") * lax.axis_size("y"), 64, 0)
    t_1 = to_column(t_row, one_hot(rows, LANES, upper))
    t_2 = to_column(t_row, one_hot(rows, LANES, upper + 32))
    hot = one_hot(rows, stats_ref.shape[1], col * rows)
    mean, inv = to_column(stats_ref[0:1], hot), to_column(stats_ref[1:2], hot)
    for j in range(tiles):
        d_gain_ref[tile(j)] = tot[last + j, :]
        x = x_ref[:, tile(j)].astype(F32)
        out_ref[:, tile(j)] = (x + tot[j * rows : (j + 1) * rows, :]).astype(BF16)
        xhat = (x - mean) * inv
        d_xhat = tot[(tiles + j) * rows : (tiles + j + 1) * rows, :] * gain[:, tile(j)]
        grad = (d_xhat - t_1 / model_width - xhat * t_2 / model_width) * inv
        grad_ref[:, tile(j)] = (cot_ref[:, tile(j)].astype(F32) + grad).astype(BF16)


def shards(tokens_in, gain, w_qkv, qk_gain, w_up, w_attn_out, w_down, cotangent):
    rows_c, width = tokens_in.shape
    n_col = lax.axis_size(COL)
    n_z = lax.axis_size("z")
    tokens = rows_c * n_col
    rows = tokens // (2 * n_z)
    model_width = width * lax.axis_size(ROW)
    swap = [(0, 1), (1, 0)]
    hidden_w = w_up.shape[1]
    w_qkv3 = jnp.transpose(w_qkv, (1, 0, 2))
    in_w, out_w = 3 * LANES + hidden_w, LANES + hidden_w
    tiles = (in_w + out_w) // LANES
    f_sum = in_w // LANES * (rows + 1) + 3
    low_at = f_sum + out_w // LANES * rows
    sum_rows = -(-(low_at + 2 * rows + in_w // LANES) // 16) * 16
    row_rows = tiles * rows + 8
    col_rows = 2 * width // LANES * rows_c + width // LANES + 1

    def scratch(*dims):
        return pltpu.VMEM(dims, F32)

    (sent,) = pl.pallas_call(
        spread_kernel,
        out_shape=[shape((n_col, col_rows, LANES))],
        in_specs=[pl.BlockSpec(memory_space=pltpu.HBM)] * 2,
        out_specs=[pl.BlockSpec(memory_space=pltpu.VMEM)],
        scratch_shapes=[
            pltpu.VMEM((rows_c, width), BF16),
            pltpu.VMEM((rows_c, width), BF16),
            scratch(col_rows, LANES),
            pltpu.SemaphoreType.DMA((2,)),
        ],
    )(tokens_in, cotangent)
    got = lax.all_to_all(sent, COL, 0, 0)

    weights = (gain, w_qkv3, w_up, w_attn_out, w_down)
    work = [
        scratch(tokens // 2 + 8, in_w),
        scratch(tokens // 2 + 8, 2 * LANES),
        scratch(tokens // 2, out_w),
        scratch(tokens // 2, LANES),
        scratch(n_z, sum_rows, LANES),
    ]
    other, x_all, cot_all = call(
        lambda *refs: other_kernel(rows, *refs),
        [shape((n_z, sum_rows, LANES)), shape((tokens, width)), shape((tokens, width))],
        [scratch(tokens, width), scratch(tokens, width)] + work,
        got,
        *weights,
    )
    (own,) = call(
        lambda *refs: own_kernel(rows, *refs),
        [shape((n_z, sum_rows, LANES), F32)],
        work,
        x_all,
        cot_all,
        *weights,
    )
    (half,) = call(
        lambda *refs: add_kernel(rows, f_sum, low_at, *refs),
        [shape((n_z, sum_rows, LANES))],
        [scratch(sum_rows, LANES)],
        own,
        lax.ppermute(other, "core", swap),
    )
    got = lax.all_to_all(half, "z", 0, 0)

    sent, c_vec = call(
        lambda *refs: row_kernel(model_width, rows, f_sum, low_at, *refs),
        [shape((n_z, row_rows, LANES)), shape((16, LANES), F32)],
        [scratch(sum_rows, LANES), scratch(row_rows, LANES)],
        got,
        qk_gain,
    )
    mine = lax.all_to_all(sent, "z", 0, 0)
    theirs = lax.ppermute(mine, "core", swap)
    half, half_cols, half_part = call(
        lambda *refs: unpack_kernel(rows, *refs),
        [
            shape((tokens // 2, in_w + out_w)),
            shape((tokens // 2, LANES), F32),
            shape((tokens // 2, 2 * width), F32),
        ],
        [scratch(tokens // 2, in_w + out_w)],
        mine,
        w_down,
        w_up,
    )

    sent, d_qk_gain, attended, hidden, d_qkv, d_up, normed, stats = call(
        lambda *refs: attention_kernel(rows, *refs),
        [
            shape((n_col, col_rows, LANES)),
            shape((2, LANES), F32),
            shape((tokens, LANES)),
            shape((tokens, hidden_w)),
            shape((tokens, 3 * LANES)),
            shape((tokens, hidden_w)),
            shape((tokens, width)),
            shape((2, width), F32),
        ],
        [
            pltpu.VMEM((tokens, in_w + out_w), BF16),
            scratch(tokens // 2, in_w + out_w),
            scratch(n_col, col_rows, LANES),
            scratch(tokens // 2, LANES),
            scratch(tokens, LANES),
            scratch(tokens, 2 * width),
        ],
        half,
        half_cols,
        half_part,
        theirs,
        c_vec,
        x_all,
        gain,
        qk_gain,
        w_qkv3,
        w_up,
        w_attn_out,
        w_down,
    )
    got = lax.all_to_all(sent, COL, 0, 0)
    d_w_attn_out = dot(attended, cot_all, TN).astype(BF16)
    d_w_down = dot(hidden, cot_all, TN).astype(BF16)
    d_w_qkv = dot(normed, d_qkv, TN).astype(BF16).reshape(w_qkv.shape)
    d_w_up = dot(normed, d_up, TN).astype(BF16)
    layer_out, token_grad, d_gain, d_qk_gain = call(
        lambda *refs: finish_kernel(model_width, *refs),
        [
            shape((rows_c, width)),
            shape((rows_c, width)),
            shape((width,), F32),
            shape((2, LANES), F32),
        ],
        [scratch(col_rows, LANES)],
        got,
        stats,
        tokens_in,
        cotangent,
        gain,
        d_qk_gain,
    )
    return (
        layer_out,
        token_grad,
        d_gain,
        d_w_qkv,
        d_qk_gain,
        d_w_up,
        d_w_attn_out,
        d_w_down,
    )


def solution(mesh):
    fine = Mesh(mesh.devices.reshape(-1, 2, 4, 8), ("z", "core", "x", "y"))
    in_specs = (
        P(COL, ROW),
        P(ROW),
        P(ROW, None, COL),
        P(None, COL),
        P(ROW, COL),
        P(COL, ROW),
        P(COL, ROW),
        P(COL, ROW),
    )
    out_specs = (
        P(COL, ROW),
        P(COL, ROW),
        P(ROW),
        P(ROW, None, COL),
        P(None, COL),
        P(ROW, COL),
        P(COL, ROW),
        P(COL, ROW),
    )
    return jax.shard_map(shards, mesh=fine, in_specs=in_specs, out_specs=out_specs, check_vma=False)
```

```python
import jax
import jax.numpy as jnp
from jax import lax
from jax.experimental import pallas as pl
from jax.experimental.pallas import tpu as pltpu
from jax.sharding import Mesh
from jax.sharding import PartitionSpec as P

LANES = 128
EPS = 1e-06
ROW = ("z", "core")
COL = ("x", "y")
F32 = jnp.float32
BF16 = jnp.bfloat16

NN = (((1,), (0,)), ((), ()))
NT = (((1,), (1,)), ((), ()))
TN = (((0,), (0,)), ((), ()))


def dot(a, b, dims):
    return lax.dot_general(a, b, dims, preferred_element_type=F32)


def split(values, parts):
    out = []
    for _ in range(parts):
        high = values.astype(BF16).astype(F32)
        out.append(high)
        values = values - high
    return out


def one_hot(rows, lanes, first):
    lane = lax.broadcasted_iota(jnp.int32, (rows, lanes), 1)
    return lane == lax.broadcasted_iota(jnp.int32, (rows, lanes), 0) + first


def to_column(row, hot):
    return jnp.sum(jnp.where(hot, row, 0.0), 1, keepdims=True)


def to_row(column, hot):
    return jnp.sum(jnp.where(hot, column, 0.0), 0, keepdims=True)


def two_to_row(a, b, rows):
    out = jnp.zeros((1, LANES), F32)
    for at, part in zip((0, 32, 64, 96), split(a, 2) + split(b, 2)):
        out = out + to_row(part, one_hot(rows, LANES, at))
    return out


def two_to_columns(row, rows):
    first = one_hot(rows, LANES, 0) | one_hot(rows, LANES, 32)
    second = one_hot(rows, LANES, 64) | one_hot(rows, LANES, 96)
    return to_column(row, first), to_column(row, second)


def tile(j):
    return slice(j * LANES, (j + 1) * LANES)


def call(kernel, outs, scratch, *args):
    return pl.pallas_call(
        kernel,
        out_shape=outs,
        in_specs=[pl.BlockSpec(memory_space=pltpu.VMEM)] * len(args),
        out_specs=[pl.BlockSpec(memory_space=pltpu.VMEM)] * len(outs),
        scratch_shapes=scratch,
        compiler_params=pltpu.CompilerParams(vmem_limit_bytes=16 * 2**20),
    )(*args)


def shape(dims, dtype=BF16):
    return jax.ShapeDtypeStruct(dims, dtype)


def spread_kernel(x_hbm, cot_hbm, out_ref, x_ref, cot_ref, block, sems):
    copies = [
        pltpu.make_async_copy(x_hbm, x_ref, sems.at[0]),
        pltpu.make_async_copy(cot_hbm, cot_ref, sems.at[1]),
    ]
    for copy in copies:
        copy.start()
    block[...] = jnp.zeros_like(block)
    rows, width = x_ref.shape
    at = 0
    for copy, ref in zip(copies, (x_ref, cot_ref)):
        copy.wait()
        values = ref[...].astype(F32)
        for j in range(width // LANES):
            block[at : at + rows, :] = values[:, tile(j)]
            at += rows
    out_ref[...] = jnp.broadcast_to(block[...].astype(BF16)[None], out_ref.shape)


def gather_kernel(got_ref, x_ref, cot_ref, xs, cs):
    n_col, width = got_ref.shape[0], x_ref.shape[1]
    rows = x_ref.shape[0] // n_col
    tiles = width // LANES
    for c in range(n_col):
        values = got_ref[c].astype(F32)
        here = slice(c * rows, (c + 1) * rows)
        for j in range(tiles):
            xs[here, tile(j)] = values[j * rows : (j + 1) * rows]
            cs[here, tile(j)] = values[(tiles + j) * rows : (tiles + j + 1) * rows]
    x_ref[...] = xs[...].astype(BF16)
    cot_ref[...] = cs[...].astype(BF16)


def products(
    which, rows, x_ref, cot_ref, gain_ref, wq_ref, wu_ref, wa_ref, wd_ref, out_ref, ps, fs, gs, st, lay
):
    width = x_ref.shape[1]
    n_z = out_ref.shape[0]
    half = n_z * rows
    mine = pl.ds(pl.multiple_of(which * half, 16), half)
    x = x_ref[mine, :].astype(F32)
    cot = cot_ref[mine, :]
    f_tiles, b_tiles = ps.shape[1] // LANES, gs.shape[1] // LANES
    f_sum = f_tiles * (rows + 1) + 3
    gain = gain_ref[...].reshape(1, width)
    gains = jnp.concatenate(split(gain, 3) + [jnp.zeros((5, width), F32)], 0)
    scaled = jnp.concatenate([x * gain, gains], 0)
    xg = scaled.astype(BF16)
    xg_low = (scaled - xg.astype(F32)).astype(BF16)
    fine = []
    for j in range(2):
        p = dot(xg, wq_ref[j], NN) + dot(xg_low, wq_ref[j], NN)
        ps[:, tile(j)] = p.astype(BF16).astype(F32)
        fs[:, tile(j)] = p - ps[:, tile(j)]
        fine.append(jnp.sum(p[half:], 0, keepdims=True))
    ps[:, tile(2)] = dot(xg, wq_ref[2], NN)
    ps[:, 3 * LANES :] = dot(xg, wu_ref[...], NN)
    gs[:, 0 : wa_ref.shape[0]] = dot(cot, wa_ref[...], NT)
    gs[:, wa_ref.shape[0] :] = dot(cot, wd_ref[...], NT)
    c_vec = jnp.sum(ps[half:, :], 0, keepdims=True)
    s_1 = jnp.sum(x, 1, keepdims=True)
    s_2 = jnp.sum(x * x, 1, keepdims=True)
    lane = lax.broadcasted_iota(jnp.int32, (half, LANES), 1)
    place = lax.rem(lax.broadcasted_iota(jnp.int32, (half, LANES), 0), rows)
    st[...] = jnp.where(lane == place, s_1, 0.0) + jnp.where(lane == place + 32, s_2, 0.0)
    c_rows = jnp.concatenate(fine + [c_vec[:, tile(j)] for j in range(2, f_tiles)], 0)
    c_high, c_low = split(c_rows[0:3], 2)
    c_rows = jnp.concatenate([c_high, c_rows[3:]], 0)
    low_at = f_sum + b_tiles * rows
    fill = jnp.zeros((lay.shape[1] - low_at - 2 * rows - 3, LANES), F32)
    c_low = jnp.concatenate([c_low, fill], 0)
    for d in range(n_z):
        at = slice(d * rows, (d + 1) * rows)
        for j in range(f_tiles):
            lay[d, j * rows : (j + 1) * rows, :] = ps[at, tile(j)]
        stat = jnp.sum(st[at, :], 0, keepdims=True)
        lay[d, f_tiles * rows : f_sum, :] = jnp.concatenate([c_rows] + split(stat, 3), 0)
        for j in range(b_tiles):
            lay[d, f_sum + j * rows : f_sum + (j + 1) * rows, :] = gs[at, tile(j)]
        for j in range(2):
            lay[d, low_at + j * rows : low_at + (j + 1) * rows, :] = fs[at, tile(j)]
        lay[d, low_at + 2 * rows :, :] = c_low
    out_ref[...] = lay[...].astype(out_ref.dtype)


def other_kernel(rows, got_ref, gain_ref, wq_ref, wu_ref, wa_ref, wd_ref, out_ref, x_ref, cot_ref, xs, cs, *scr):
    gather_kernel(got_ref, x_ref, cot_ref, xs, cs)
    other = 1 - lax.axis_index("core")
    products(other, rows, x_ref, cot_ref, gain_ref, wq_ref, wu_ref, wa_ref, wd_ref, out_ref, *scr)


def own_kernel(rows, x_ref, cot_ref, gain_ref, wq_ref, wu_ref, wa_ref, wd_ref, out_ref, *scr):
    core = lax.axis_index("core")
    products(core, rows, x_ref, cot_ref, gain_ref, wq_ref, wu_ref, wa_ref, wd_ref, out_ref, *scr)


def fine_pairs(rows, f_sum, low_at):
    c_at, c_low_at = f_sum // (rows + 1) * rows, low_at + 2 * rows
    return (
        (slice(0, 2 * rows), slice(low_at, low_at + 2 * rows)),
        (slice(c_at, c_at + 3), slice(c_low_at, c_low_at + 3)),
    )


def add_kernel(rows, f_sum, low_at, own_ref, came_ref, out_ref, block):
    for d in range(own_ref.shape[0]):
        block[...] = own_ref[d] + came_ref[d].astype(F32)
        for high, low in fine_pairs(rows, f_sum, low_at):
            whole = block[high, :] + block[low, :]
            block[high, :] = whole.astype(BF16).astype(F32)
            block[low, :] = whole - block[high, :]
        stat = jnp.sum(block[f_sum - 3 : f_sum, :], 0, keepdims=True)
        block[f_sum - 3 : f_sum, :] = jnp.concatenate(split(stat, 3), 0)
        out_ref[d] = block[...].astype(BF16)


def gelu_parts(x):
    c = 0.7978845608028654
    t = jnp.tanh(c * (x + 0.044715 * (x * x * x)))
    half = 0.5 * (1.0 + t)
    slope = half + 0.5 * x * (1.0 - t * t) * (c * (1.0 + 3 * 0.044715 * (x * x)))
    return x * half, slope


def sum_blocks(got_ref, tot):
    total = got_ref[0].astype(F32)
    for d in range(1, got_ref.shape[0]):
        total = total + got_ref[d].astype(F32)
    tot[...] = total


def row_kernel(
    model_width, rows, f_sum, low_at, got_ref, qk_gain_ref, out_ref, c_ref, tot, block
):
    sum_blocks(got_ref, tot)
    for high, low in fine_pairs(rows, f_sum, low_at):
        tot[high, :] = tot[high, :] + tot[low, :]
    tiles = (f_sum - 3) // (rows + 1)
    c_ref[0:tiles, :] = tot[tiles * rows : tiles * rows + tiles, :]
    c_ref[tiles:, :] = jnp.zeros((c_ref.shape[0] - tiles, LANES), F32)
    stat = jnp.sum(tot[f_sum - 3 : f_sum, :], 0, keepdims=True)
    mean = to_column(stat, one_hot(rows, LANES, 0)) / model_width
    var = to_column(stat, one_hot(rows, LANES, 32)) / model_width - mean * mean
    inv = lax.rsqrt(var + EPS)

    def merged(j):
        return (tot[j * rows : (j + 1) * rows, :] - mean * c_ref[j : j + 1, :]) * inv

    def norm(j):
        values = merged(j)
        average = jnp.mean(values, -1, keepdims=True)
        centred = values - average
        rstd = lax.rsqrt(jnp.mean(centred * centred, -1, keepdims=True) + EPS)
        return centred * rstd * qk_gain_ref[j : j + 1], rstd, average

    block[0:rows, :], rstd_q, mean_q = norm(0)
    block[rows : 2 * rows, :], rstd_k, mean_k = norm(1)
    block[2 * rows : 3 * rows, :] = merged(2)
    back = tiles * rows
    block[back : back + rows, :] = tot[f_sum : f_sum + rows, :]
    s_1 = jnp.zeros((rows, LANES), F32)
    s_2 = jnp.zeros((rows, LANES), F32)
    for j in range(3, tiles):
        up = merged(j)
        hidden, slope = gelu_parts(up)
        block[j * rows : (j + 1) * rows, :] = hidden
        at = (j - 2) * rows
        d_hidden = tot[f_sum + at : f_sum + at + rows, :].astype(BF16).astype(F32)
        d_up = (d_hidden * slope).astype(BF16).astype(F32)
        block[back + at : back + at + rows, :] = d_up
        s_1 = s_1 + d_up * c_ref[j : j + 1, :]
        s_2 = s_2 + d_up * up
    s_1 = jnp.sum(s_1, 1, keepdims=True)
    s_2 = jnp.sum(s_2, 1, keepdims=True)
    last = (2 * tiles - 2) * rows
    pairs = ((rstd_q, rstd_k), (mean_q, mean_k), (mean, inv), (s_1, s_2))
    block[last:, :] = jnp.concatenate(
        [two_to_row(a, b, rows) for a, b in pairs]
        + [jnp.zeros((block.shape[0] - last - len(pairs), LANES), F32)],
        0,
    )
    out_ref[...] = jnp.broadcast_to(block[...].astype(BF16)[None], out_ref.shape)


def unpack(rows, ref, half, cols):
    tiles = half.shape[-1] // LANES
    lane = lax.broadcasted_iota(jnp.int32, (rows, LANES), 1)
    for d in range(ref.shape[0]):
        values = ref[d].astype(F32)
        at = slice(d * rows, (d + 1) * rows)
        for j in range(tiles):
            half[at, tile(j)] = values[j * rows : (j + 1) * rows]
        scalars = jnp.zeros((rows, LANES), F32)
        for i in range(4):
            a, b = two_to_columns(values[tiles * rows + i : tiles * rows + i + 1], rows)
            scalars = jnp.where(lane == 2 * i, a, scalars)
            scalars = jnp.where(lane == 2 * i + 1, b, scalars)
        cols[at, :] = scalars


def mlp_products(values, wd_ref, wu_ref, part_ref, at):
    hidden_w, width = wd_ref.shape
    f_width = 3 * LANES + hidden_w
    part_ref[at, 0:width] = dot(values[:, 3 * LANES : f_width], wd_ref[...], NN)
    part_ref[at, width:] = dot(values[:, f_width + LANES :], wu_ref[...], NT)


def unpack_kernel(rows, mine_ref, wd_ref, wu_ref, out_ref, cols_ref, part_ref, half):
    unpack(rows, mine_ref, half, cols_ref)
    out_ref[...] = half[...].astype(BF16)
    mlp_products(out_ref[...], wd_ref, wu_ref, part_ref, slice(None))


def attention_kernel(
    rows, half_ref, half_cols_ref, half_part_ref, theirs_ref, c_ref, x_ref, gain_ref, qk_gain_ref, wq_ref, wu_ref, wa_ref, wd_ref,
    send_ref, d_gain_ref, att_ref, hidden_ref, d_qkv_ref, d_up_ref, normed_ref, stats_ref,
    full, wide, block, cols, cols_ref, mlp
):
    tokens, width = x_ref.shape
    half = tokens // 2
    core = lax.axis_index("core")
    f_width = 3 * LANES + hidden_ref.shape[1]
    unpack(rows, theirs_ref, wide, cols)
    for h, values, scalars in ((core, half_ref, half_cols_ref), (1 - core, wide, cols)):
        at = pl.ds(pl.multiple_of(h * half, 16), half)
        full[at, :] = values[...].astype(BF16)
        cols_ref[at, :] = scalars[...]
    mlp[pl.ds(pl.multiple_of(core * half, 16), half), :] = half_part_ref[...]
    other = pl.ds(pl.multiple_of((1 - core) * half, 16), half)
    mlp_products(wide[...].astype(BF16), wd_ref, wu_ref, mlp, other)

    def whole(at, size):
        return full[:, at : at + size]

    def scalar(i):
        return cols_ref[:, i : i + 1]

    hidden_ref[...] = whole(3 * LANES, hidden_ref.shape[1])
    d_up_ref[...] = whole(f_width + LANES, d_up_ref.shape[1])
    q, k, v = (whole(j * LANES, LANES) for j in range(3))
    d_att = whole(f_width, LANES)
    mean, inv = scalar(4), scalar(5)
    hot = one_hot(tokens, stats_ref.shape[1], 0)
    stats_ref[...] = jnp.concatenate([to_row(mean, hot), to_row(inv, hot)], 0)

    scale = LANES ** (-0.5)
    scores = dot(q, k, NT) * scale
    probs = jnp.exp(scores - jnp.max(scores, -1, keepdims=True))
    probs = probs * (1.0 / jnp.sum(probs, -1, keepdims=True))
    low = probs.astype(BF16)
    attended = dot(low, v, NN).astype(BF16)
    att_ref[...] = attended
    branch = dot(attended, wa_ref[...], NN) + mlp[:, 0:width]
    wide[:, 0:width] = branch[0:half]
    wide[:, width : 2 * width] = branch[half:]
    d_probs = dot(d_att, v, NT)
    delta = jnp.sum(probs * d_probs, -1, keepdims=True)
    d_scores = (probs * (d_probs - delta)).astype(BF16)
    d_qn = dot(d_scores, k, NN) * scale
    d_kn = dot(d_scores, q, TN) * scale
    d_v = dot(low, d_att, TN).astype(BF16)

    def back(rows_low, i, g, d_rows):
        rstd, average = scalar(i), scalar(i + 2)
        unit = rows_low.astype(F32) * (1.0 / g)
        d_unit = d_rows * g
        d_values = (
            d_unit
            - jnp.mean(d_unit, -1, keepdims=True)
            - unit * jnp.mean(d_unit * unit, -1, keepdims=True)
        ) * rstd
        return d_values.astype(BF16), jnp.sum(d_rows * unit, 0, keepdims=True), unit * (1.0 / rstd) + average

    d_q, g_q, query = back(q, 0, qk_gain_ref[0:1], d_qn)
    d_k, g_k, key = back(k, 1, qk_gain_ref[1:2], d_kn)
    d_gain_ref[0:1, :] = g_q
    d_gain_ref[1:2, :] = g_k
    d_qkv_ref[:, tile(0)] = d_q
    d_qkv_ref[:, tile(1)] = d_k
    d_qkv_ref[:, tile(2)] = d_v
    d_normed = mlp[:, width:]
    for j, d_j in enumerate((d_q, d_k, d_v)):
        d_normed += dot(d_j, wq_ref[j], NT)
    wide[:, 2 * width : 3 * width] = d_normed[0:half]
    wide[:, 3 * width : 4 * width] = d_normed[half:]
    d_qf, d_kf, d_vf = d_q.astype(F32), d_k.astype(F32), d_v.astype(F32)
    t_1 = scalar(6)
    t_1 += jnp.sum(d_qf * c_ref[0:1] + d_kf * c_ref[1:2] + d_vf * c_ref[2:3], 1, keepdims=True)
    t_2 = scalar(7)
    t_2 += jnp.sum(d_qf * query + d_kf * key + d_vf * v.astype(F32), 1, keepdims=True)
    xhat = (x_ref[...].astype(F32) - mean) * inv
    normed_ref[...] = (xhat * gain_ref[...].reshape(1, width)).astype(BF16)
    part = jnp.sum(d_normed * xhat, 0, keepdims=True)
    n_col = send_ref.shape[0]
    rows_c = tokens // n_col
    lane = lax.broadcasted_iota(jnp.int32, (tokens, LANES), 1)
    place = lax.rem(lax.broadcasted_iota(jnp.int32, (tokens, LANES), 0), rows_c)
    ts = jnp.where(lane == place, t_1, 0.0) + jnp.where(lane == place + 32, t_2, 0.0)
    cols[...] = ts[0:half] + pltpu.roll(ts[half:], 64, 1)

    w_tiles = width // LANES
    used = 2 * w_tiles * rows_c
    part = jnp.concatenate([part[:, tile(j)] for j in range(w_tiles)], 0)
    for c in range(n_col):
        h, at = divmod(c * rows_c, half)
        at = slice(at, at + rows_c)
        for i in range(2):
            for j in range(w_tiles):
                to = (i * w_tiles + j) * rows_c
                block[c, to : to + rows_c, :] = wide[at, tile((2 * i + h) * w_tiles + j)]
        t_row = jnp.sum(cols[at, :], 0, keepdims=True)
        block[c, used : used + w_tiles + 1, :] = jnp.concatenate([part, t_row], 0)
    send_ref[...] = block[...].astype(BF16)


def finish_kernel(
    model_width, got_ref, stats_ref, x_ref, cot_ref, gain_ref, d_qk_ref,
    out_ref, grad_ref, d_gain_ref, d_qk_out, tot
):
    gain = gain_ref[...].reshape(1, x_ref.shape[1])
    d_qk_out[...] = d_qk_ref[...]
    sum_blocks(got_ref, tot)
    rows, width = x_ref.shape
    tiles = width // LANES
    last = 2 * rows * tiles
    t_row = tot[last + tiles : last + tiles + 1, :]
    col = lax.axis_index("x") * lax.axis_size("y") + lax.axis_index("y")
    upper = jnp.where(col * 2 >= lax.axis_size("x") * lax.axis_size("y"), 64, 0)
    t_1 = to_column(t_row, one_hot(rows, LANES, upper))
    t_2 = to_column(t_row, one_hot(rows, LANES, upper + 32))
    hot = one_hot(rows, stats_ref.shape[1], col * rows)
    mean, inv = to_column(stats_ref[0:1], hot), to_column(stats_ref[1:2], hot)
    for j in range(tiles):
        d_gain_ref[tile(j)] = tot[last + j, :]
        x = x_ref[:, tile(j)].astype(F32)
        out_ref[:, tile(j)] = (x + tot[j * rows : (j + 1) * rows, :]).astype(BF16)
        xhat = (x - mean) * inv
        d_xhat = tot[(tiles + j) * rows : (tiles + j + 1) * rows, :] * gain[:, tile(j)]
        grad = (d_xhat - t_1 / model_width - xhat * t_2 / model_width) * inv
        grad_ref[:, tile(j)] = (cot_ref[:, tile(j)].astype(F32) + grad).astype(BF16)


def shards(tokens_in, gain, w_qkv, qk_gain, w_up, w_attn_out, w_down, cotangent):
    rows_c, width = tokens_in.shape
    n_col = lax.axis_size(COL)
    n_z = lax.axis_size("z")
    tokens = rows_c * n_col
    rows = tokens // (2 * n_z)
    model_width = width * lax.axis_size(ROW)
    swap = [(0, 1), (1, 0)]
    hidden_w = w_up.shape[1]
    w_qkv3 = jnp.transpose(w_qkv, (1, 0, 2))
    in_w, out_w = 3 * LANES + hidden_w, LANES + hidden_w
    tiles = (in_w + out_w) // LANES
    f_sum = in_w // LANES * (rows + 1) + 3
    low_at = f_sum + out_w // LANES * rows
    sum_rows = -(-(low_at + 2 * rows + 3) // 8) * 8
    row_rows = tiles * rows + 8
    col_rows = 2 * width // LANES * rows_c + width // LANES + 1

    def scratch(*dims):
        return pltpu.VMEM(dims, F32)

    (sent,) = pl.pallas_call(
        spread_kernel,
        out_shape=[shape((n_col, col_rows, LANES))],
        in_specs=[pl.BlockSpec(memory_space=pltpu.HBM)] * 2,
        out_specs=[pl.BlockSpec(memory_space=pltpu.VMEM)],
        scratch_shapes=[
            pltpu.VMEM((rows_c, width), BF16),
            pltpu.VMEM((rows_c, width), BF16),
            scratch(col_rows, LANES),
            pltpu.SemaphoreType.DMA((2,)),
        ],
    )(tokens_in, cotangent)
    got = lax.all_to_all(sent, COL, 0, 0)

    weights = (gain, w_qkv3, w_up, w_attn_out, w_down)
    work = [
        scratch(tokens // 2 + 8, in_w),
        scratch(tokens // 2 + 8, 2 * LANES),
        scratch(tokens // 2, out_w),
        scratch(tokens // 2, LANES),
        scratch(n_z, sum_rows, LANES),
    ]
    other, x_all, cot_all = call(
        lambda *refs: other_kernel(rows, *refs),
        [shape((n_z, sum_rows, LANES)), shape((tokens, width)), shape((tokens, width))],
        [scratch(tokens, width), scratch(tokens, width)] + work,
        got,
        *weights,
    )
    (own,) = call(
        lambda *refs: own_kernel(rows, *refs),
        [shape((n_z, sum_rows, LANES), F32)],
        work,
        x_all,
        cot_all,
        *weights,
    )
    (half,) = call(
        lambda *refs: add_kernel(rows, f_sum, low_at, *refs),
        [shape((n_z, sum_rows, LANES))],
        [scratch(sum_rows, LANES)],
        own,
        lax.ppermute(other, "core", swap),
    )
    got = lax.all_to_all(half, "z", 0, 0)

    sent, c_vec = call(
        lambda *refs: row_kernel(model_width, rows, f_sum, low_at, *refs),
        [shape((n_z, row_rows, LANES)), shape((16, LANES), F32)],
        [scratch(sum_rows, LANES), scratch(row_rows, LANES)],
        got,
        qk_gain,
    )
    mine = lax.all_to_all(sent, "z", 0, 0)
    theirs = lax.ppermute(mine, "core", swap)
    half, half_cols, half_part = call(
        lambda *refs: unpack_kernel(rows, *refs),
        [
            shape((tokens // 2, in_w + out_w)),
            shape((tokens // 2, LANES), F32),
            shape((tokens // 2, 2 * width), F32),
        ],
        [scratch(tokens // 2, in_w + out_w)],
        mine,
        w_down,
        w_up,
    )

    sent, d_qk_gain, attended, hidden, d_qkv, d_up, normed, stats = call(
        lambda *refs: attention_kernel(rows, *refs),
        [
            shape((n_col, col_rows, LANES)),
            shape((2, LANES), F32),
            shape((tokens, LANES)),
            shape((tokens, hidden_w)),
            shape((tokens, 3 * LANES)),
            shape((tokens, hidden_w)),
            shape((tokens, width)),
            shape((2, width), F32),
        ],
        [
            pltpu.VMEM((tokens, in_w + out_w), BF16),
            scratch(tokens // 2, in_w + out_w),
            scratch(n_col, col_rows, LANES),
            scratch(tokens // 2, LANES),
            scratch(tokens, LANES),
            scratch(tokens, 2 * width),
        ],
        half,
        half_cols,
        half_part,
        theirs,
        c_vec,
        x_all,
        gain,
        qk_gain,
        w_qkv3,
        w_up,
        w_attn_out,
        w_down,
    )
    got = lax.all_to_all(sent, COL, 0, 0)
    d_w_attn_out = dot(attended, cot_all, TN).astype(BF16)
    d_w_down = dot(hidden, cot_all, TN).astype(BF16)
    d_w_qkv = dot(normed, d_qkv, TN).astype(BF16).reshape(w_qkv.shape)
    d_w_up = dot(normed, d_up, TN).astype(BF16)
    layer_out, token_grad, d_gain, d_qk_gain = call(
        lambda *refs: finish_kernel(model_width, *refs),
        [
            shape((rows_c, width)),
            shape((rows_c, width)),
            shape((width,), F32),
            shape((2, LANES), F32),
        ],
        [scratch(col_rows, LANES)],
        got,
        stats,
        tokens_in,
        cotangent,
        gain,
        d_qk_gain,
    )
    return (
        layer_out,
        token_grad,
        d_gain,
        d_w_qkv,
        d_qk_gain,
        d_w_up,
        d_w_attn_out,
        d_w_down,
    )


def solution(mesh):
    fine = Mesh(mesh.devices.reshape(-1, 2, 4, 8), ("z", "core", "x", "y"))
    in_specs = (
        P(COL, ROW),
        P(ROW),
        P(ROW, None, COL),
        P(None, COL),
        P(ROW, COL),
        P(COL, ROW),
        P(COL, ROW),
        P(COL, ROW),
    )
    out_specs = (
        P(COL, ROW),
        P(COL, ROW),
        P(ROW),
        P(ROW, None, COL),
        P(None, COL),
        P(ROW, COL),
        P(COL, ROW),
        P(COL, ROW),
    )
    return jax.shard_map(shards, mesh=fine, in_specs=in_specs, out_specs=out_specs, check_vma=False)
```

```python
import jax
import jax.numpy as jnp
from jax import lax
from jax.experimental import pallas as pl
from jax.experimental.pallas import tpu as pltpu
from jax.sharding import Mesh
from jax.sharding import PartitionSpec as P

LANES = 128
EPS = 1e-06
ROW = ("z", "core")
COL = ("x", "y")
F32 = jnp.float32
BF16 = jnp.bfloat16

NN = (((1,), (0,)), ((), ()))
NT = (((1,), (1,)), ((), ()))
TN = (((0,), (0,)), ((), ()))


def dot(a, b, dims):
    return lax.dot_general(a, b, dims, preferred_element_type=F32)


def split(values, parts):
    out = []
    for _ in range(parts):
        high = values.astype(BF16).astype(F32)
        out.append(high)
        values = values - high
    return out


def one_hot(rows, lanes, first):
    lane = lax.broadcasted_iota(jnp.int32, (rows, lanes), 1)
    return lane == lax.broadcasted_iota(jnp.int32, (rows, lanes), 0) + first


def to_column(row, hot):
    return jnp.sum(jnp.where(hot, row, 0.0), 1, keepdims=True)


def to_row(column, hot):
    return jnp.sum(jnp.where(hot, column, 0.0), 0, keepdims=True)


def two_to_row(a, b, rows):
    out = jnp.zeros((1, LANES), F32)
    for at, part in zip((0, 32, 64, 96), split(a, 2) + split(b, 2)):
        out = out + to_row(part, one_hot(rows, LANES, at))
    return out


def two_to_columns(row, rows):
    first = one_hot(rows, LANES, 0) | one_hot(rows, LANES, 32)
    second = one_hot(rows, LANES, 64) | one_hot(rows, LANES, 96)
    return to_column(row, first), to_column(row, second)


def tile(j):
    return slice(j * LANES, (j + 1) * LANES)


def call(kernel, outs, scratch, *args):
    return pl.pallas_call(
        kernel,
        out_shape=outs,
        in_specs=[pl.BlockSpec(memory_space=pltpu.VMEM)] * len(args),
        out_specs=[pl.BlockSpec(memory_space=pltpu.VMEM)] * len(outs),
        scratch_shapes=scratch,
        compiler_params=pltpu.CompilerParams(vmem_limit_bytes=16 * 2**20),
    )(*args)


def shape(dims, dtype=BF16):
    return jax.ShapeDtypeStruct(dims, dtype)


def spread_kernel(x_hbm, cot_hbm, out_ref, x_ref, cot_ref, block, sems):
    copies = [
        pltpu.make_async_copy(x_hbm, x_ref, sems.at[0]),
        pltpu.make_async_copy(cot_hbm, cot_ref, sems.at[1]),
    ]
    for copy in copies:
        copy.start()
    block[...] = jnp.zeros_like(block)
    rows, width = x_ref.shape
    at = 0
    for copy, ref in zip(copies, (x_ref, cot_ref)):
        copy.wait()
        values = ref[...].astype(F32)
        for j in range(width // LANES):
            block[at : at + rows, :] = values[:, tile(j)]
            at += rows
    out_ref[...] = jnp.broadcast_to(block[...].astype(BF16)[None], out_ref.shape)


def gather_kernel(got_ref, x_ref, cot_ref, xs, cs):
    n_col, width = got_ref.shape[0], x_ref.shape[1]
    rows = x_ref.shape[0] // n_col
    tiles = width // LANES
    for c in range(n_col):
        values = got_ref[c].astype(F32)
        here = slice(c * rows, (c + 1) * rows)
        for j in range(tiles):
            xs[here, tile(j)] = values[j * rows : (j + 1) * rows]
            cs[here, tile(j)] = values[(tiles + j) * rows : (tiles + j + 1) * rows]
    x_ref[...] = xs[...].astype(BF16)
    cot_ref[...] = cs[...].astype(BF16)


def products(
    which, rows, x_ref, cot_ref, gain_ref, wq_ref, wu_ref, wa_ref, wd_ref, out_ref, ps, fs, gs, st, lay
):
    width = x_ref.shape[1]
    n_z = out_ref.shape[0]
    half = n_z * rows
    mine = pl.ds(pl.multiple_of(which * half, 16), half)
    x = x_ref[mine, :].astype(F32)
    cot = cot_ref[mine, :]
    f_tiles, b_tiles = ps.shape[1] // LANES, gs.shape[1] // LANES
    f_sum = f_tiles * (rows + 1) + 3
    gain = gain_ref[...].reshape(1, width)
    gains = jnp.concatenate(split(gain, 3) + [jnp.zeros((5, width), F32)], 0)
    scaled = jnp.concatenate([x * gain, gains], 0)
    xg = scaled.astype(BF16)
    xg_low = (scaled - xg.astype(F32)).astype(BF16)
    fine = []
    for j in range(2):
        p = dot(xg, wq_ref[j], NN) + dot(xg_low, wq_ref[j], NN)
        ps[:, tile(j)] = p.astype(BF16).astype(F32)
        fs[:, tile(j)] = p - ps[:, tile(j)]
        fine.append(jnp.sum(p[half:], 0, keepdims=True))
    ps[:, tile(2)] = dot(xg, wq_ref[2], NN)
    ps[:, 3 * LANES :] = dot(xg, wu_ref[...], NN)
    gs[:, 0 : wa_ref.shape[0]] = dot(cot, wa_ref[...], NT)
    gs[:, wa_ref.shape[0] :] = dot(cot, wd_ref[...], NT)
    c_vec = jnp.sum(ps[half:, :], 0, keepdims=True)
    s_1 = jnp.sum(x, 1, keepdims=True)
    s_2 = jnp.sum(x * x, 1, keepdims=True)
    lane = lax.broadcasted_iota(jnp.int32, (half, LANES), 1)
    place = lax.rem(lax.broadcasted_iota(jnp.int32, (half, LANES), 0), rows)
    st[...] = jnp.where(lane == place, s_1, 0.0) + jnp.where(lane == place + 32, s_2, 0.0)
    c_rows = jnp.concatenate(fine + [c_vec[:, tile(j)] for j in range(2, f_tiles)], 0)
    c_high, c_low = split(c_rows[0:3], 2)
    c_rows = jnp.concatenate([c_high, c_rows[3:]], 0)
    low_at = f_sum + b_tiles * rows
    fine_at = lay.shape[1] - 2 * rows
    fill = jnp.zeros((fine_at - low_at - 3, LANES), F32)
    c_low = jnp.concatenate([c_low, fill], 0)
    for d in range(n_z):
        at = slice(d * rows, (d + 1) * rows)
        for j in range(f_tiles):
            lay[d, j * rows : (j + 1) * rows, :] = ps[at, tile(j)]
        stat = jnp.sum(st[at, :], 0, keepdims=True)
        lay[d, f_tiles * rows : f_sum, :] = jnp.concatenate([c_rows] + split(stat, 3), 0)
        for j in range(b_tiles):
            lay[d, f_sum + j * rows : f_sum + (j + 1) * rows, :] = gs[at, tile(j)]
        for j in range(2):
            lay[d, fine_at + j * rows : fine_at + (j + 1) * rows, :] = fs[at, tile(j)]
        lay[d, low_at:fine_at, :] = c_low
    out_ref[...] = lay[...].astype(out_ref.dtype)


def other_kernel(rows, got_ref, gain_ref, wq_ref, wu_ref, wa_ref, wd_ref, out_ref, x_ref, cot_ref, xs, cs, *scr):
    gather_kernel(got_ref, x_ref, cot_ref, xs, cs)
    other = 1 - lax.axis_index("core")
    products(other, rows, x_ref, cot_ref, gain_ref, wq_ref, wu_ref, wa_ref, wd_ref, out_ref, *scr)


def own_kernel(rows, x_ref, cot_ref, gain_ref, wq_ref, wu_ref, wa_ref, wd_ref, out_ref, *scr):
    core = lax.axis_index("core")
    products(core, rows, x_ref, cot_ref, gain_ref, wq_ref, wu_ref, wa_ref, wd_ref, out_ref, *scr)


def gain_parts(rows, f_sum, low_at):
    c_at = f_sum // (rows + 1) * rows
    return slice(c_at, c_at + 3), slice(low_at, low_at + 3)


def add_kernel(rows, f_sum, low_at, own_ref, came_ref, out_ref, block):
    length = out_ref.shape[1]
    high, low = gain_parts(rows, f_sum, low_at)
    for d in range(own_ref.shape[0]):
        block[...] = own_ref[d] + came_ref[d].astype(F32)
        block[0 : 2 * rows, :] = block[0 : 2 * rows, :] + block[length:, :]
        whole = block[high, :] + block[low, :]
        block[high, :] = whole.astype(BF16).astype(F32)
        block[low, :] = whole - block[high, :]
        stat = jnp.sum(block[f_sum - 3 : f_sum, :], 0, keepdims=True)
        block[f_sum - 3 : f_sum, :] = jnp.concatenate(split(stat, 3), 0)
        out_ref[d] = block[0:length, :].astype(BF16)


def gelu_parts(x):
    c = 0.7978845608028654
    t = jnp.tanh(c * (x + 0.044715 * (x * x * x)))
    half = 0.5 * (1.0 + t)
    slope = half + 0.5 * x * (1.0 - t * t) * (c * (1.0 + 3 * 0.044715 * (x * x)))
    return x * half, slope


def sum_blocks(got_ref, tot):
    total = got_ref[0].astype(F32)
    for d in range(1, got_ref.shape[0]):
        total = total + got_ref[d].astype(F32)
    tot[...] = total


def row_kernel(
    model_width, rows, f_sum, low_at, got_ref, qk_gain_ref, out_ref, c_ref, tot, block
):
    sum_blocks(got_ref, tot)
    high, low = gain_parts(rows, f_sum, low_at)
    tot[high, :] = tot[high, :] + tot[low, :]
    tiles = (f_sum - 3) // (rows + 1)
    c_ref[0:tiles, :] = tot[tiles * rows : tiles * rows + tiles, :]
    c_ref[tiles:, :] = jnp.zeros((c_ref.shape[0] - tiles, LANES), F32)
    stat = jnp.sum(tot[f_sum - 3 : f_sum, :], 0, keepdims=True)
    mean = to_column(stat, one_hot(rows, LANES, 0)) / model_width
    var = to_column(stat, one_hot(rows, LANES, 32)) / model_width - mean * mean
    inv = lax.rsqrt(var + EPS)

    def merged(j):
        return (tot[j * rows : (j + 1) * rows, :] - mean * c_ref[j : j + 1, :]) * inv

    def norm(j):
        values = merged(j)
        average = jnp.mean(values, -1, keepdims=True)
        centred = values - average
        rstd = lax.rsqrt(jnp.mean(centred * centred, -1, keepdims=True) + EPS)
        return centred * rstd * qk_gain_ref[j : j + 1], rstd, average

    block[0:rows, :], rstd_q, mean_q = norm(0)
    block[rows : 2 * rows, :], rstd_k, mean_k = norm(1)
    block[2 * rows : 3 * rows, :] = merged(2)
    back = tiles * rows
    block[back : back + rows, :] = tot[f_sum : f_sum + rows, :]
    s_1 = jnp.zeros((rows, LANES), F32)
    s_2 = jnp.zeros((rows, LANES), F32)
    for j in range(3, tiles):
        up = merged(j)
        hidden, slope = gelu_parts(up)
        block[j * rows : (j + 1) * rows, :] = hidden
        at = (j - 2) * rows
        d_hidden = tot[f_sum + at : f_sum + at + rows, :].astype(BF16).astype(F32)
        d_up = (d_hidden * slope).astype(BF16).astype(F32)
        block[back + at : back + at + rows, :] = d_up
        s_1 = s_1 + d_up * c_ref[j : j + 1, :]
        s_2 = s_2 + d_up * up
    s_1 = jnp.sum(s_1, 1, keepdims=True)
    s_2 = jnp.sum(s_2, 1, keepdims=True)
    last = (2 * tiles - 2) * rows
    pairs = ((rstd_q, rstd_k), (mean_q, mean_k), (mean, inv), (s_1, s_2))
    block[last:, :] = jnp.concatenate(
        [two_to_row(a, b, rows) for a, b in pairs]
        + [jnp.zeros((block.shape[0] - last - len(pairs), LANES), F32)],
        0,
    )
    out_ref[...] = jnp.broadcast_to(block[...].astype(BF16)[None], out_ref.shape)


def unpack(rows, ref, half, cols):
    tiles = half.shape[-1] // LANES
    lane = lax.broadcasted_iota(jnp.int32, (rows, LANES), 1)
    for d in range(ref.shape[0]):
        values = ref[d].astype(F32)
        at = slice(d * rows, (d + 1) * rows)
        for j in range(tiles):
            half[at, tile(j)] = values[j * rows : (j + 1) * rows]
        scalars = jnp.zeros((rows, LANES), F32)
        for i in range(4):
            a, b = two_to_columns(values[tiles * rows + i : tiles * rows + i + 1], rows)
            scalars = jnp.where(lane == 2 * i, a, scalars)
            scalars = jnp.where(lane == 2 * i + 1, b, scalars)
        cols[at, :] = scalars


def mlp_products(values, wd_ref, wu_ref, part_ref, at):
    hidden_w, width = wd_ref.shape
    f_width = 3 * LANES + hidden_w
    part_ref[at, 0:width] = dot(values[:, 3 * LANES : f_width], wd_ref[...], NN)
    part_ref[at, width:] = dot(values[:, f_width + LANES :], wu_ref[...], NT)


def unpack_kernel(rows, mine_ref, wd_ref, wu_ref, out_ref, cols_ref, part_ref, half):
    unpack(rows, mine_ref, half, cols_ref)
    out_ref[...] = half[...].astype(BF16)
    mlp_products(out_ref[...], wd_ref, wu_ref, part_ref, slice(None))


def attention_kernel(
    rows, half_ref, half_cols_ref, half_part_ref, theirs_ref, c_ref, x_ref, gain_ref, qk_gain_ref, wq_ref, wu_ref, wa_ref, wd_ref,
    send_ref, d_gain_ref, att_ref, hidden_ref, d_qkv_ref, d_up_ref, normed_ref, stats_ref,
    full, wide, block, cols, cols_ref, mlp
):
    tokens, width = x_ref.shape
    half = tokens // 2
    core = lax.axis_index("core")
    f_width = 3 * LANES + hidden_ref.shape[1]
    unpack(rows, theirs_ref, wide, cols)
    for h, values, scalars in ((core, half_ref, half_cols_ref), (1 - core, wide, cols)):
        at = pl.ds(pl.multiple_of(h * half, 16), half)
        full[at, :] = values[...].astype(BF16)
        cols_ref[at, :] = scalars[...]
    mlp[pl.ds(pl.multiple_of(core * half, 16), half), :] = half_part_ref[...]
    other = pl.ds(pl.multiple_of((1 - core) * half, 16), half)
    mlp_products(wide[...].astype(BF16), wd_ref, wu_ref, mlp, other)

    def whole(at, size):
        return full[:, at : at + size]

    def scalar(i):
        return cols_ref[:, i : i + 1]

    hidden_ref[...] = whole(3 * LANES, hidden_ref.shape[1])
    d_up_ref[...] = whole(f_width + LANES, d_up_ref.shape[1])
    q, k, v = (whole(j * LANES, LANES) for j in range(3))
    d_att = whole(f_width, LANES)
    mean, inv = scalar(4), scalar(5)
    hot = one_hot(tokens, stats_ref.shape[1], 0)
    stats_ref[...] = jnp.concatenate([to_row(mean, hot), to_row(inv, hot)], 0)

    scale = LANES ** (-0.5)
    scores = dot(q, k, NT) * scale
    probs = jnp.exp(scores - jnp.max(scores, -1, keepdims=True))
    probs = probs * (1.0 / jnp.sum(probs, -1, keepdims=True))
    low = probs.astype(BF16)
    attended = dot(low, v, NN).astype(BF16)
    att_ref[...] = attended
    branch = dot(attended, wa_ref[...], NN) + mlp[:, 0:width]
    wide[:, 0:width] = branch[0:half]
    wide[:, width : 2 * width] = branch[half:]
    d_probs = dot(d_att, v, NT)
    delta = jnp.sum(probs * d_probs, -1, keepdims=True)
    d_scores = (probs * (d_probs - delta)).astype(BF16)
    d_qn = dot(d_scores, k, NN) * scale
    d_kn = dot(d_scores, q, TN) * scale
    d_v = dot(low, d_att, TN).astype(BF16)

    def back(rows_low, i, g, d_rows):
        rstd, average = scalar(i), scalar(i + 2)
        unit = rows_low.astype(F32) * (1.0 / g)
        d_unit = d_rows * g
        d_values = (
            d_unit
            - jnp.mean(d_unit, -1, keepdims=True)
            - unit * jnp.mean(d_unit * unit, -1, keepdims=True)
        ) * rstd
        return d_values.astype(BF16), jnp.sum(d_rows * unit, 0, keepdims=True), unit * (1.0 / rstd) + average

    d_q, g_q, query = back(q, 0, qk_gain_ref[0:1], d_qn)
    d_k, g_k, key = back(k, 1, qk_gain_ref[1:2], d_kn)
    d_gain_ref[0:1, :] = g_q
    d_gain_ref[1:2, :] = g_k
    d_qkv_ref[:, tile(0)] = d_q
    d_qkv_ref[:, tile(1)] = d_k
    d_qkv_ref[:, tile(2)] = d_v
    d_normed = mlp[:, width:]
    for j, d_j in enumerate((d_q, d_k, d_v)):
        d_normed += dot(d_j, wq_ref[j], NT)
    wide[:, 2 * width : 3 * width] = d_normed[0:half]
    wide[:, 3 * width : 4 * width] = d_normed[half:]
    d_qf, d_kf, d_vf = d_q.astype(F32), d_k.astype(F32), d_v.astype(F32)
    t_1 = scalar(6)
    t_1 += jnp.sum(d_qf * c_ref[0:1] + d_kf * c_ref[1:2] + d_vf * c_ref[2:3], 1, keepdims=True)
    t_2 = scalar(7)
    t_2 += jnp.sum(d_qf * query + d_kf * key + d_vf * v.astype(F32), 1, keepdims=True)
    xhat = (x_ref[...].astype(F32) - mean) * inv
    normed_ref[...] = (xhat * gain_ref[...].reshape(1, width)).astype(BF16)
    part = jnp.sum(d_normed * xhat, 0, keepdims=True)
    n_col = send_ref.shape[0]
    rows_c = tokens // n_col
    lane = lax.broadcasted_iota(jnp.int32, (tokens, LANES), 1)
    place = lax.rem(lax.broadcasted_iota(jnp.int32, (tokens, LANES), 0), rows_c)
    ts = jnp.where(lane == place, t_1, 0.0) + jnp.where(lane == place + 32, t_2, 0.0)
    cols[...] = ts[0:half] + pltpu.roll(ts[half:], 64, 1)

    w_tiles = width // LANES
    used = 2 * w_tiles * rows_c
    part = jnp.concatenate([part[:, tile(j)] for j in range(w_tiles)], 0)
    for c in range(n_col):
        h, at = divmod(c * rows_c, half)
        at = slice(at, at + rows_c)
        for i in range(2):
            for j in range(w_tiles):
                to = (i * w_tiles + j) * rows_c
                block[c, to : to + rows_c, :] = wide[at, tile((2 * i + h) * w_tiles + j)]
        t_row = jnp.sum(cols[at, :], 0, keepdims=True)
        block[c, used : used + w_tiles + 1, :] = jnp.concatenate([part, t_row], 0)
    send_ref[...] = block[...].astype(BF16)


def finish_kernel(
    model_width, got_ref, stats_ref, x_ref, cot_ref, gain_ref, d_qk_ref,
    out_ref, grad_ref, d_gain_ref, d_qk_out, tot
):
    gain = gain_ref[...].reshape(1, x_ref.shape[1])
    d_qk_out[...] = d_qk_ref[...]
    sum_blocks(got_ref, tot)
    rows, width = x_ref.shape
    tiles = width // LANES
    last = 2 * rows * tiles
    t_row = tot[last + tiles : last + tiles + 1, :]
    col = lax.axis_index("x") * lax.axis_size("y") + lax.axis_index("y")
    upper = jnp.where(col * 2 >= lax.axis_size("x") * lax.axis_size("y"), 64, 0)
    t_1 = to_column(t_row, one_hot(rows, LANES, upper))
    t_2 = to_column(t_row, one_hot(rows, LANES, upper + 32))
    hot = one_hot(rows, stats_ref.shape[1], col * rows)
    mean, inv = to_column(stats_ref[0:1], hot), to_column(stats_ref[1:2], hot)
    for j in range(tiles):
        d_gain_ref[tile(j)] = tot[last + j, :]
        x = x_ref[:, tile(j)].astype(F32)
        out_ref[:, tile(j)] = (x + tot[j * rows : (j + 1) * rows, :]).astype(BF16)
        xhat = (x - mean) * inv
        d_xhat = tot[(tiles + j) * rows : (tiles + j + 1) * rows, :] * gain[:, tile(j)]
        grad = (d_xhat - t_1 / model_width - xhat * t_2 / model_width) * inv
        grad_ref[:, tile(j)] = (cot_ref[:, tile(j)].astype(F32) + grad).astype(BF16)


def shards(tokens_in, gain, w_qkv, qk_gain, w_up, w_attn_out, w_down, cotangent):
    rows_c, width = tokens_in.shape
    n_col = lax.axis_size(COL)
    n_z = lax.axis_size("z")
    tokens = rows_c * n_col
    rows = tokens // (2 * n_z)
    model_width = width * lax.axis_size(ROW)
    swap = [(0, 1), (1, 0)]
    hidden_w = w_up.shape[1]
    w_qkv3 = jnp.transpose(w_qkv, (1, 0, 2))
    in_w, out_w = 3 * LANES + hidden_w, LANES + hidden_w
    tiles = (in_w + out_w) // LANES
    f_sum = in_w // LANES * (rows + 1) + 3
    low_at = f_sum + out_w // LANES * rows
    z_rows = -(-(low_at + 3) // 16) * 16
    sum_rows = z_rows + 2 * rows
    row_rows = tiles * rows + 8
    col_rows = 2 * width // LANES * rows_c + width // LANES + 1

    def scratch(*dims):
        return pltpu.VMEM(dims, F32)

    (sent,) = pl.pallas_call(
        spread_kernel,
        out_shape=[shape((n_col, col_rows, LANES))],
        in_specs=[pl.BlockSpec(memory_space=pltpu.HBM)] * 2,
        out_specs=[pl.BlockSpec(memory_space=pltpu.VMEM)],
        scratch_shapes=[
            pltpu.VMEM((rows_c, width), BF16),
            pltpu.VMEM((rows_c, width), BF16),
            scratch(col_rows, LANES),
            pltpu.SemaphoreType.DMA((2,)),
        ],
    )(tokens_in, cotangent)
    got = lax.all_to_all(sent, COL, 0, 0)

    weights = (gain, w_qkv3, w_up, w_attn_out, w_down)
    work = [
        scratch(tokens // 2 + 8, in_w),
        scratch(tokens // 2 + 8, 2 * LANES),
        scratch(tokens // 2, out_w),
        scratch(tokens // 2, LANES),
        scratch(n_z, sum_rows, LANES),
    ]
    other, x_all, cot_all = call(
        lambda *refs: other_kernel(rows, *refs),
        [shape((n_z, sum_rows, LANES)), shape((tokens, width)), shape((tokens, width))],
        [scratch(tokens, width), scratch(tokens, width)] + work,
        got,
        *weights,
    )
    (own,) = call(
        lambda *refs: own_kernel(rows, *refs),
        [shape((n_z, sum_rows, LANES), F32)],
        work,
        x_all,
        cot_all,
        *weights,
    )
    (half,) = call(
        lambda *refs: add_kernel(rows, f_sum, low_at, *refs),
        [shape((n_z, z_rows, LANES))],
        [scratch(sum_rows, LANES)],
        own,
        lax.ppermute(other, "core", swap),
    )
    got = lax.all_to_all(half, "z", 0, 0)

    sent, c_vec = call(
        lambda *refs: row_kernel(model_width, rows, f_sum, low_at, *refs),
        [shape((n_z, row_rows, LANES)), shape((16, LANES), F32)],
        [scratch(z_rows, LANES), scratch(row_rows, LANES)],
        got,
        qk_gain,
    )
    mine = lax.all_to_all(sent, "z", 0, 0)
    theirs = lax.ppermute(mine, "core", swap)
    half, half_cols, half_part = call(
        lambda *refs: unpack_kernel(rows, *refs),
        [
            shape((tokens // 2, in_w + out_w)),
            shape((tokens // 2, LANES), F32),
            shape((tokens // 2, 2 * width), F32),
        ],
        [scratch(tokens // 2, in_w + out_w)],
        mine,
        w_down,
        w_up,
    )

    sent, d_qk_gain, attended, hidden, d_qkv, d_up, normed, stats = call(
        lambda *refs: attention_kernel(rows, *refs),
        [
            shape((n_col, col_rows, LANES)),
            shape((2, LANES), F32),
            shape((tokens, LANES)),
            shape((tokens, hidden_w)),
            shape((tokens, 3 * LANES)),
            shape((tokens, hidden_w)),
            shape((tokens, width)),
            shape((2, width), F32),
        ],
        [
            pltpu.VMEM((tokens, in_w + out_w), BF16),
            scratch(tokens // 2, in_w + out_w),
            scratch(n_col, col_rows, LANES),
            scratch(tokens // 2, LANES),
            scratch(tokens, LANES),
            scratch(tokens, 2 * width),
        ],
        half,
        half_cols,
        half_part,
        theirs,
        c_vec,
        x_all,
        gain,
        qk_gain,
        w_qkv3,
        w_up,
        w_attn_out,
        w_down,
    )
    got = lax.all_to_all(sent, COL, 0, 0)
    d_w_attn_out = dot(attended, cot_all, TN).astype(BF16)
    d_w_down = dot(hidden, cot_all, TN).astype(BF16)
    d_w_qkv = dot(normed, d_qkv, TN).astype(BF16).reshape(w_qkv.shape)
    d_w_up = dot(normed, d_up, TN).astype(BF16)
    layer_out, token_grad, d_gain, d_qk_gain = call(
        lambda *refs: finish_kernel(model_width, *refs),
        [
            shape((rows_c, width)),
            shape((rows_c, width)),
            shape((width,), F32),
            shape((2, LANES), F32),
        ],
        [scratch(col_rows, LANES)],
        got,
        stats,
        tokens_in,
        cotangent,
        gain,
        d_qk_gain,
    )
    return (
        layer_out,
        token_grad,
        d_gain,
        d_w_qkv,
        d_qk_gain,
        d_w_up,
        d_w_attn_out,
        d_w_down,
    )


def solution(mesh):
    fine = Mesh(mesh.devices.reshape(-1, 2, 4, 8), ("z", "core", "x", "y"))
    in_specs = (
        P(COL, ROW),
        P(ROW),
        P(ROW, None, COL),
        P(None, COL),
        P(ROW, COL),
        P(COL, ROW),
        P(COL, ROW),
        P(COL, ROW),
    )
    out_specs = (
        P(COL, ROW),
        P(COL, ROW),
        P(ROW),
        P(ROW, None, COL),
        P(None, COL),
        P(ROW, COL),
        P(COL, ROW),
        P(COL, ROW),
    )
    return jax.shard_map(shards, mesh=fine, in_specs=in_specs, out_specs=out_specs, check_vma=False)
```
